512 devices in a mesh: tok: 32 (over z, x_hi), ch: 16 (over x_lo, y, core).
Axes of the slice: x: 4 (x_hi: 2, x_lo: 2; x = x_hi * 2 + x_lo), y: 4, z: 16, core: 2. Of those that a mesh axis runs over, the one named last changes fastest.
Arguments:
- tokens: bfloat16 [4096, 4096], P('tok', 'ch'), may hold values from -6 to 6
- w_input: bfloat16 [4096, 8192], P('tok', 'ch'), may hold values from -0.09375 to 0.09375
- cotangent: bfloat16 [4096, 8192], P('tok', 'ch'), may hold values from -6 to 6
- b_state: bfloat16 [8, 4096, 128], P(None, 'tok'), may hold values from -0.1875 to 0.1875
- c_state: bfloat16 [8, 4096, 128], P(None, 'tok'), may hold values from -0.1875 to 0.1875
- step_raw: float32 [128, 4096], P('ch', 'tok'), as said below
- rate_log: float32 [128], P('ch'), as said below
- skip_gain: float32 [128], P('ch'), may hold values from 0.5 to 1.5
Outputs:
- token_grad: bfloat16 [4096, 4096], P('tok', 'ch')
- weight_grad: bfloat16 [4096, 8192], P('tok', 'ch')
- step_grad: float32 [128, 4096], P('ch', 'tok')
- output_map_grad: float32 [8, 4096, 128], P(None, 'tok')
The draws below stay inside these ranges and needn't reach their ends.
Inputs may be any that keep to these rules, and one draw needn't show every extreme that they name: `rate_log`: every value lies between log(0.3 / 4096) and log(0.05). `step_raw`: every value lies between -2.5 and 3.5.
All inputs are finite; a program needn't handle non-finite values.
Results may differ from the reference program's by a relative error of at most 0.025.
Values may be sent and summed in bfloat16 or wider, within the bound.
A program may use at most 128 MiB of HBM per device.

```python
import jax
import jax.numpy as jnp
from jax import lax

D = 4096
HEADS = 128
HEAD_DIM = 64
N_STATE = 128
GROUPS = 8
TOK_DEV = 128
TOKENS = 4096
INNER = 8192
N_TOK = 32
N_CH = 16


def draw_step_raw(key, part):
    key = jax.random.fold_in(key, 11)
    first, second = jax.random.split(key)
    blocks = TOKENS // TOK_DEV
    levels = jax.random.uniform(first, (HEADS, blocks), jnp.float32, -2.5, 3.0)
    levels = jnp.repeat(levels, TOK_DEV, axis=1)
    noise = 0.35 * jax.random.normal(second, (HEADS, TOKENS), jnp.float32)
    return jnp.clip(levels + noise, -2.5, 3.5)


def draw_rate_log(key, part):
    key = jax.random.fold_in(key, 23)
    low = jnp.log(0.3 / TOKENS)
    high = jnp.log(0.05)
    first = jax.random.fold_in(key, 0)
    values = jax.random.uniform(first, (HEADS,), jnp.float32, low, high)
    return values


def shard_levels(rng, dims, cuts, least, top_value):
    def one(position, parts):
        draws = jax.random.uniform(jax.random.fold_in(jax.random.fold_in(rng, 6), position), (parts,), jnp.float32, least / len(cuts), top_value / len(cuts))
        return jnp.repeat(jnp.exp(draws), dims[position] // parts).reshape((-1,) + (1,) * (len(dims) - position - 1))

    factor_of = one(*cuts[0])
    for cut in cuts[1:]:
        factor_of = factor_of * one(*cut)
    return factor_of


def bell_draw(rng, dims, scale, most, cuts=(), dtype=jnp.bfloat16):
    loudness = shard_levels(rng, dims, cuts, -0.22, 0.18) if cuts else 1.0
    result = jax.random.normal(rng, dims, jnp.float32) * scale * loudness
    return jnp.minimum(jnp.maximum(result, -most), most).astype(dtype)


def setup_inputs(seed: int = 0) -> dict:
    key_list = jax.random.split(jax.random.key(seed), 9)
    return {
        "tokens": bell_draw(key_list[0], (TOKENS, D), 1.0, 6.0, ((0, 32), (1, 16))),
        "w_input": bell_draw(key_list[1], (D, INNER), D ** -0.5, 0.09375, ((0, 32), (1, 16))),
        "cotangent": bell_draw(key_list[2], (TOKENS, INNER), 1.0, 6.0, ((0, 32), (1, 16))),
        "b_state": bell_draw(key_list[3], (GROUPS, TOKENS, N_STATE), (8 * N_STATE) ** -0.5, 0.1875, ((1, 32),)),
        "c_state": bell_draw(key_list[4], (GROUPS, TOKENS, N_STATE), (8 * N_STATE) ** -0.5, 0.1875, ((1, 32),)),
        "step_raw": draw_step_raw(jax.random.fold_in(key_list[8], 71), 0),
        "rate_log": draw_rate_log(jax.random.fold_in(key_list[8], 71), 0),
        "skip_gain": jnp.clip(0.5 + 1.0 * jax.random.uniform(key_list[7], (HEADS,), jnp.float32) ** shard_levels(key_list[7], (HEADS,), ((0, 16),), -0.2, 0.2), 0.5, 1.5),
    }


highest = lax.Precision.HIGHEST


def block_local(inputs_h, grad_h, b_heads, c_heads, steps, rates):
    log_decay = jnp.cumsum(steps * rates[:, None], axis=1)
    log_total = log_decay[:, -1:]
    end_weight = jnp.exp(log_total - log_decay) * steps
    block_decay = jnp.exp(log_total[:, 0])
    state_local = jnp.einsum('lhp,hl,hln->hpn', inputs_h, end_weight, b_heads, precision=highest)
    adjoint_local = jnp.einsum('lhp,hl,hln->hpn', grad_h, jnp.exp(log_decay), c_heads, precision=highest)
    return block_decay, state_local, adjoint_local


def block_grads(inputs_h, grad_h, b_heads, c_heads, steps, step_raw, rates, skip_gain, state_in, adjoint_in):
    length = steps.shape[1]
    log_decay = jnp.cumsum(steps * rates[:, None], axis=1)
    log_total = log_decay[:, -1:]
    end_weight = jnp.exp(log_total - log_decay) * steps
    row_ids = jnp.arange(length)[:, None]
    col_ids = jnp.arange(length)[None, :]
    lower_mask = row_ids >= col_ids
    log_gap = log_decay[:, :, None] - log_decay[:, None, :]
    decay_mat = jnp.where(lower_mask[None], jnp.exp(jnp.minimum(log_gap, 0.0)), 0.0)
    intersection = jnp.einsum('hrn,hsn->hrs', c_heads, b_heads, precision=highest)
    kernel = decay_mat * intersection
    adjoint_b = jnp.einsum('hpn,hsn->shp', adjoint_in, b_heads, precision=highest)
    back_proj = jnp.einsum('hrs,rhp->shp', kernel, grad_h, precision=highest)
    back_proj = back_proj + jnp.exp(log_total - log_decay).T[:, :, None] * adjoint_b
    input_grad = skip_gain[None, :, None] * grad_h + steps.T[:, :, None] * back_proj
    input_term = jnp.sum(inputs_h * back_proj, axis=-1).T
    cross = jnp.einsum('rhp,shp->hrs', grad_h, inputs_h, precision=highest)
    pair_weights = decay_mat * steps[:, None, :] * cross
    map_local = jnp.einsum('hts,hsn->htn', pair_weights, b_heads, precision=highest)
    state_g = jnp.einsum('hpn,thp->htn', state_in, grad_h, precision=highest)
    map_heads = map_local + jnp.exp(log_decay)[:, :, None] * state_g
    pair_terms = kernel * steps[:, None, :] * cross
    upper_ones = (col_ids >= row_ids).astype(jnp.float32)
    strict_lower = (col_ids < row_ids).astype(jnp.float32)
    tail_sums = jnp.einsum('tr,hrs->hts', upper_ones, pair_terms, precision=highest)
    pair_part = jnp.sum(tail_sums * strict_lower[None], axis=-1)
    state_c = jnp.einsum('hpn,hrn->rhp', state_in, c_heads, precision=highest)
    start_terms = jnp.exp(log_decay) * jnp.sum(grad_h * state_c, axis=-1).T
    start_part = jnp.einsum('tr,hr->ht', upper_ones, start_terms, precision=highest)
    end_terms = end_weight * jnp.sum(inputs_h * adjoint_b, axis=-1).T
    end_part = jnp.einsum('ts,hs->ht', strict_lower, end_terms, precision=highest)
    corner = jnp.exp(log_total[:, 0]) * jnp.sum(adjoint_in * state_in, axis=(1, 2))
    decay_term = pair_part + start_part + end_part + corner[:, None]
    step_grad = jax.nn.sigmoid(step_raw) * (input_term + rates[:, None] * decay_term)
    return input_grad, step_grad, map_heads


def reference(tokens, w_input, cotangent, b_state, c_state, step_raw, rate_log, skip_gain):
    blocks = N_TOK
    length = TOK_DEV
    per_group = HEADS // GROUPS
    inputs = jnp.dot(tokens, w_input, preferred_element_type=jnp.float32).astype(jnp.bfloat16)
    inputs_all = inputs.astype(jnp.float32).reshape(blocks, length, HEADS, HEAD_DIM)
    grad_all = cotangent.astype(jnp.float32).reshape(blocks, length, HEADS, HEAD_DIM)
    b_blocks = b_state.astype(jnp.float32).reshape(GROUPS, blocks, length, N_STATE).transpose(1, 0, 2, 3)
    c_blocks = c_state.astype(jnp.float32).reshape(GROUPS, blocks, length, N_STATE).transpose(1, 0, 2, 3)
    raw_blocks = step_raw.reshape(HEADS, blocks, length).transpose(1, 0, 2)
    steps_blocks = jax.nn.softplus(raw_blocks)
    rates = -jnp.exp(rate_log)

    def local_fn(items):
        inputs_h, grad_h, b_group, c_group, steps = items
        b_heads = jnp.repeat(b_group, per_group, axis=0)
        c_heads = jnp.repeat(c_group, per_group, axis=0)
        return block_local(inputs_h, grad_h, b_heads, c_heads, steps, rates)

    block_decay, state_local, adjoint_local = lax.map(local_fn, (inputs_all, grad_all, b_blocks, c_blocks, steps_blocks))

    def forward_step(carry, items):
        decay_now, state_now = items
        return decay_now[:, None, None] * carry + state_now, carry

    zero_state = jnp.zeros((HEADS, HEAD_DIM, N_STATE), jnp.float32)
    _, states_in = lax.scan(forward_step, zero_state, (block_decay, state_local))

    def backward_step(carry, items):
        decay_now, adjoint_now = items
        return decay_now[:, None, None] * carry + adjoint_now, carry

    _, adjoints_in = lax.scan(backward_step, zero_state, (block_decay, adjoint_local), reverse=True)

    def grad_fn(items):
        inputs_h, grad_h, b_group, c_group, steps, raw, state_in, adjoint_in = items
        b_heads = jnp.repeat(b_group, per_group, axis=0)
        c_heads = jnp.repeat(c_group, per_group, axis=0)
        input_grad, step_grad, map_heads = block_grads(inputs_h, grad_h, b_heads, c_heads, steps, raw, rates, skip_gain, state_in, adjoint_in)
        map_group = jnp.sum(map_heads.reshape(GROUPS, per_group, length, N_STATE), axis=1)
        return input_grad, step_grad, map_group

    input_grad, step_grad, map_group = lax.map(grad_fn, (inputs_all, grad_all, b_blocks, c_blocks, steps_blocks, raw_blocks, states_in, adjoints_in))
    input_grad = input_grad.reshape(TOKENS, INNER).astype(jnp.bfloat16)
    step_grad = step_grad.transpose(1, 0, 2).reshape(HEADS, TOKENS)
    output_map_grad = map_group.transpose(1, 0, 2, 3).reshape(GROUPS, TOKENS, N_STATE)
    width = INNER // N_CH
    total = jnp.zeros((TOKENS, D), jnp.float32)
    for index in range(N_CH):
        part = jnp.dot(input_grad[:, index * width:(index + 1) * width], w_input[:, index * width:(index + 1) * width].T, preferred_element_type=jnp.float32).astype(jnp.bfloat16)
        part = lax.optimization_barrier(part)
        total = total + part.astype(jnp.float32)
    token_grad = total.astype(jnp.bfloat16)
    weight_grad = jnp.dot(tokens.T, input_grad, preferred_element_type=jnp.float32).astype(jnp.bfloat16)
    return token_grad, weight_grad, step_grad, output_map_grad
```

```python
import jax
import jax.numpy as jnp
from jax import lax
from jax.experimental import pallas as pl
from jax.experimental.pallas import tpu as pltpu
from jax.sharding import PartitionSpec as P

MESH = pl.DeviceIdType.MESH
HIGHEST = lax.Precision.HIGHEST
F32 = jnp.float32
BF16 = jnp.bfloat16
TOK = 128
HEAD = 64
HALF = 4
CH = HALF * HEAD
STATE = 128

NN = (((1,), (0,)), ((), ()))
NT = (((1,), (1,)), ((), ()))


def dot(a, b, dims=NN):
    return lax.dot_general(a, b, dims, preferred_element_type=F32)


def dot2(a, b, dims=NN):
    high = a.astype(BF16)
    low = (a - high.astype(F32)).astype(BF16)
    return dot(high, b, dims) + dot(low, b, dims)


def dot_exact(a, b):
    return lax.dot_general(a, b, NN, precision=HIGHEST, preferred_element_type=F32)


def heads_to_rows(rows, p):
    return jnp.concatenate(
        [
            jnp.broadcast_to(rows[p * HALF + i : p * HALF + i + 1], (HEAD, rows.shape[1]))
            for i in range(HALF)
        ],
        axis=0,
    )


def kernel(
    nz,
    nk,
    tokens,
    w,
    cot,
    b_in,
    c_in,
    raw_in,
    rate_log,
    skip_in,
    token_grad,
    weight_grad,
    step_grad,
    map_grad,
    feat,
    wg,
    ig,
    tcol,
    g,
    bs,
    cs,
    raw,
    dtile,
    dall,
    send_state,
    recv_state,
    back_state,
    state_in,
    adj_in,
    gte,
    gtb,
    xtb,
    dec,
    inter,
    back_local,
    abt,
    a_last,
    s_first,
    vecs,
    igtm,
    y_all,
    y_sib,
    y_out,
    y_in,
    m_own,
    m_in,
    m_groups,
    s_out,
    s_swap,
    wgrad,
    local_sem,
    send_sem,
    recv_sem,
):
    tok, c = lax.axis_index("tok"), lax.axis_index("ch")
    z, r = tok // 2, tok % 2
    k, core = c // 2, c % 2
    piece = CH // nz
    rowt = TOK // nk
    chips = 2 * nk

    def ztok(zz, rr):
        return lax.rem(zz + nz, nz) * 2 + rr

    def xor(a, b, n):
        out, bit = 0, 1
        while bit < n:
            pa, pb = (a // bit) % 2, (b // bit) % 2
            out = out + bit * ((pa + pb) % 2)
            bit *= 2
        return out

    def chip(j):
        return (r + j // nk) % 2, xor(k, j % nk, nk)

    slots = {}
    used = [0]

    def slot(name, n):
        if name not in slots:
            slots[name] = used[0]
            used[0] += n
        return slots[name]

    def remote(src, dst, s, tok_to, ch_to):
        return pltpu.make_async_remote_copy(
            src_ref=src,
            dst_ref=dst,
            send_sem=send_sem.at[s],
            recv_sem=recv_sem.at[s],
            device_id=(tok_to, ch_to),
            device_id_type=MESH,
        )

    def each(first, last, f):
        def body(j, carry):
            f(j)
            return carry

        lax.fori_loop(first, last, body, 0)

    class Family:
        def __init__(self, name, first, last, make):
            self.base, self.first, self.last = slot(name, last), first, last
            self.make = lambda j: make(j, self.base + j)

        def start(self):
            each(self.first, self.last, lambda j: self.make(j).start())

        def start_one(self, j):
            self.make(j).start()

        def recv(self):
            each(self.first, self.last, lambda j: self.make(j).wait_recv())

        def recv_one(self, j):
            self.make(j).wait_recv()

        def sent(self):
            each(self.first, self.last, lambda j: self.make(j).wait_send())

    class Ring:
        def __init__(self, name, buf):
            self.base = slot(name, 4 * (nz // 2 + 1))
            self.buf = buf

        def copy(self, way, s, h):
            block = lax.rem(z - way * (s - 1) + 2 * nz, nz)
            at = self.buf.at[block, h]
            sem = self.base + (s * 2 + (0 if way == 1 else 1)) * 2 + h
            return remote(at, at, sem, ztok(z + way, r), c)

        def has(self, way, s, h):
            if s < nz // 2:
                return True
            return s == nz // 2 and h == (0 if way == 1 else 1)

        def begin(self, h):
            for way in (1, -1):
                self.copy(way, 1, h).start()

        def tick(self, s, h):
            for way in (1, -1):
                if self.has(way, s, h):
                    self.copy(way, s, h).wait_recv()
                    if self.has(way, s + 1, h):
                        self.copy(way, s + 1, h).start()

        def both(self, s):
            self.tick(s, 0)
            self.tick(s, 1)

        def sent(self):
            for s in range(1, nz // 2 + 1):
                for h in range(2):
                    for way in (1, -1):
                        if self.has(way, s, h):
                            self.copy(way, s, h).wait_send()

    barrier = pltpu.get_barrier_semaphore()

    def greet(tok_to, ch_to):
        pl.semaphore_signal(barrier, inc=1, device_id=(tok_to, ch_to), device_id_type=MESH)

    def greet_chip(j):
        rr, kk = chip(j)
        greet(z * 2 + rr, kk * 2 + core)

    each(1, nz, lambda j: greet(ztok(z + j, r), c))
    each(1, chips, greet_chip)
    greet(tok, c + 1 - 2 * core)
    greet(z * 2 + 1 - r, c + 1 - 2 * core)
    pl.semaphore_wait(barrier, (nz - 1) + (chips - 1) + 2)

    partner = z * 2 + 1 - r
    sibling = c + 1 - 2 * core
    mine = pl.ds(pl.multiple_of(r * CH, CH), CH)
    other = pl.ds(pl.multiple_of((1 - r) * CH, CH), CH)

    swap_w = remote(w.at[:, other], wg.at[z, r], slot("w", 1), partner, c)
    swap_g = remote(cot.at[:, other], g.at[r], slot("g", 1), partner, c)
    swap_b = remote(b_in.at[k], bs.at[r], slot("b", 1), partner, c)
    swap_c = remote(c_in.at[k], cs.at[r], slot("c", 1), partner, c)
    swap_r = remote(raw_in, raw.at[r], slot("r", 1), partner, c)
    for swap in (swap_r, swap_g, swap_c, swap_b, swap_w):
        swap.start()

    ring_w = Ring("ring_w", wg)
    wg[z, r] = w[:, mine]
    ring_w.begin(r)

    def feat_out(j, s):
        rr, kk = chip(j)
        return remote(tokens, feat.at[c, r], s, z * 2 + rr, kk * 2 + core)

    def feat_on(j, s):
        rr, kk = chip(j)
        at = feat.at[kk * 2 + core, rr]
        return remote(at, at, s, tok, sibling)

    feats = Family("feats", 1, chips, feat_out)
    feats_on = Family("feats_on", 0, chips, feat_on)
    feat[c, r] = tokens[...]
    feats.start()
    feats_on.start_one(0)

    g[r] = cot[:, mine]
    bs[r] = b_in[k]
    cs[r] = c_in[k]
    raw[r] = raw_in[...]
    swap_w.wait_recv()
    ring_w.begin(1 - r)
    for swap in (swap_r, swap_g, swap_c, swap_b):
        swap.wait_recv()

    low_half = r == 0
    rows = []
    for p in range(2):
        both = raw[p]
        rows.append(jnp.where(low_half, both[0:HALF], both[HALF : 2 * HALF]))
    raw8 = jnp.concatenate(rows, axis=0)
    steps = jnp.maximum(raw8, 0.0) + jnp.log1p(jnp.exp(-jnp.abs(raw8)))
    for i in range(HALF):
        rate = jnp.full((1, TOK), rate_log[0, r * HALF + i], F32)
        skip = jnp.full((1, TOK), skip_in[0, r * HALF + i], F32)
        for p in range(2):
            vecs[0, p * HALF + i : p * HALF + i + 1, :] = rate
            vecs[1, p * HALF + i : p * HALF + i + 1, :] = skip
    rates = -jnp.exp(vecs[0])
    skips = vecs[1]
    ids0 = lax.broadcasted_iota(jnp.int32, (TOK, TOK), 0)
    ids1 = lax.broadcasted_iota(jnp.int32, (TOK, TOK), 1)
    upto = (ids0 <= ids1).astype(F32)
    log_decay = dot_exact(steps * rates, upto)
    log_total = jnp.broadcast_to(log_decay[:, TOK - 1 : TOK], (2 * HALF, TOK))
    start_decay = jnp.exp(log_decay)
    end_decay = jnp.exp(log_total - log_decay)
    end_weight = end_decay * steps
    block_decay = jnp.exp(log_total)
    decay_rows = [heads_to_rows(block_decay, p) for p in range(2)]
    columns = jnp.concatenate([log_decay, jnp.zeros((TOK - 2 * HALF, TOK), F32)], axis=0).T
    dtile[...] = jnp.concatenate(
        [block_decay[0:HALF] * block_decay[HALF : 2 * HALF], jnp.zeros((HALF, TOK), F32)], axis=0
    )
    dall[z] = dtile[...]

    def decay_out(j, s):
        return remote(dtile, dall.at[z], s, ztok(z + j, r), c)

    decays = Family("decays", 1, nz, decay_out)
    decays.start()

    adjoint = []
    for p in range(2):
        gt = g[p].astype(F32).T
        gtb[p] = gt.astype(BF16)
        gte[p] = gt * heads_to_rows(start_decay, p)
        adjoint.append(dot2(gte[p], cs[p]))
    a_last[...] = adjoint[1]

    def all_to_all(name, slot_of, whole):
        send_state[slot_of] = whole.astype(BF16).reshape(nz, piece, STATE)
        recv_state[slot_of, z] = send_state[slot_of, z]

        def out(j, s):
            to = lax.rem(z + j, nz)
            return remote(
                send_state.at[slot_of, to], recv_state.at[slot_of, z], s, ztok(to, r), c
            )

        first = Family(name + "_out", 1, nz, out)
        first.start()
        return first

    def prefix(name, slot_of, target, reverse):
        head = (z * piece) // HEAD

        def hop(n, carry):
            at = nz - 1 - n if reverse else n
            back_state[slot_of, at] = carry
            return dall[at, pl.ds(head, 1), :] * carry + recv_state[slot_of, at].astype(F32)

        lax.fori_loop(0, nz, hop, jnp.zeros((piece, STATE), F32))
        target[z] = back_state[slot_of, z]

        def back(j, s):
            to = lax.rem(z + j, nz)
            return remote(back_state.at[slot_of, to], target.at[z], s, ztok(to, r), c)

        second = Family(name + "_back", 1, nz, back)
        second.start()
        return second

    adj_out = all_to_all("adj", 0, adjoint[0] + decay_rows[0] * adjoint[1])
    ring_w.both(1)

    lower = ids0 >= ids1

    def block_kernels(p):
        inter[p] = dot(cs[p], bs[p], NT)
        for i in range(HALF):
            q = p * HALF + i
            gap = columns[:, q : q + 1] - log_decay[q : q + 1, :]
            dec[q] = jnp.where(lower, jnp.exp(jnp.minimum(gap, 0.0)), 0.0)
            kern = (dec[q] * inter[p]).astype(BF16)
            back_local[p, i * HEAD : (i + 1) * HEAD, :] = dot(
                gtb[p, i * HEAD : (i + 1) * HEAD, :], kern
            )

    block_kernels(0)
    ring_w.both(2)
    block_kernels(1)
    ring_w.both(3)
    decays.recv()
    adj_out.recv()
    adj_back = prefix("adj", 0, adj_in, True)
    ring_w.both(4)
    feats.recv()
    each(1, chips, feats_on.start_one)
    if nz // 2 > 5:
        ring_w.both(5)

    def column_out(j, s):
        to = lax.rem(z + j, nz)
        src = feat.at[
            to,
            r,
            pl.ds(pl.multiple_of(k * rowt, rowt), rowt),
            pl.ds(pl.multiple_of(core * TOK, TOK), TOK),
        ]
        return remote(src, tcol.at[r, k, core, z], s, ztok(to, r), c)

    feats_on.recv()
    own_columns = pltpu.make_async_copy(
        feat.at[
            z,
            r,
            pl.ds(pl.multiple_of(k * rowt, rowt), rowt),
            pl.ds(pl.multiple_of(core * TOK, TOK), TOK),
        ],
        tcol.at[r, k, core, z],
        local_sem.at[0],
    )
    own_columns.start()
    columns_out = Family("columns", 1, nz, column_out)
    columns_out.start()

    adj_back.recv()
    ring_i = Ring("ring_i", ig)
    late = adj_in[...].reshape(CH, STATE)
    adjoint_at = [decay_rows[1] * late + a_last[...], late]
    for p in range(2):
        abt[p] = dot2(adjoint_at[p], bs[p], NT)
        back = back_local[p] + heads_to_rows(end_decay, p) * abt[p]
        grad = heads_to_rows(skips, p) * gtb[p].astype(F32) + heads_to_rows(steps, p) * back
        grad_low = grad.astype(BF16)
        ig[z, p] = grad_low
        ring_i.begin(p)
        igtm[p * TOK : (p + 1) * TOK, :] = grad_low.astype(F32).T.astype(BF16)
    for s in range(6, nz // 2 + 1):
        ring_w.both(s)
    ring_i.both(1)

    def project(n, total):
        f = feat[n].reshape(2 * TOK, CH)
        return total + dot(f, wg[n].reshape(CH, CH))

    inputs = lax.fori_loop(0, nz, project, jnp.zeros((2 * TOK, CH), F32))
    states = []
    for p in range(2):
        xt = inputs[p * TOK : (p + 1) * TOK, :].astype(BF16).astype(F32).T
        xtb[p] = xt.astype(BF16)
        states.append(dot2(xt * heads_to_rows(end_weight, p), bs[p]))
    s_first[...] = states[0]
    state_out = all_to_all("state", 1, decay_rows[1] * states[0] + states[1])

    own_columns.wait()
    columns_out.recv()

    def tcol_out(j, s):
        rr, kk = chip(j)
        at = tcol.at[r, k, core]
        return remote(at, at, s, z * 2 + rr, kk * 2 + core)

    def tcol_on(j, s):
        rr, kk = chip(j)
        at = tcol.at[rr, kk, core]
        return remote(at, at, s, tok, sibling)

    tcols = Family("tcols", 1, chips, tcol_out)
    tcols_on = Family("tcols_on", 0, chips, tcol_on)
    tcols.start()
    tcols_on.start_one(0)
    if nz // 2 > 2:
        ring_i.both(2)

    def term(kk, side):
        n = kk * 2 + side
        out = dot(igtm[...], wg[n].reshape(CH, CH), NT)
        y_all[side, kk] = out.astype(BF16).reshape(2, TOK, CH)

    def y_to_sibling(j, s):
        return remote(y_all.at[1 - core, j], y_sib.at[j], s, tok, sibling)

    y_sibs = Family("y_sib", 0, nk, y_to_sibling)

    def first_terms(j):
        term(j, 1 - core)
        y_sibs.start_one(j)

    each(0, nk, first_terms)
    if nz // 2 > 3:
        ring_i.both(3)
    each(0, nk, lambda j: term(j, core))

    state_out.recv()
    state_back = prefix("state", 1, state_in, False)

    def y_sum(j):
        y_sibs.recv_one(j)
        y_out[j] = (y_all[core, j].astype(F32) + y_sib[j].astype(F32)).astype(BF16)

    each(0, nk, y_sum)
    y_in[0] = y_out[k, r]

    def y_chip(j, s):
        rr, kk = chip(j)
        return remote(y_out.at[kk, rr], y_in.at[j], s, z * 2 + rr, kk * 2 + core)

    y_outs = Family("y_out", 1, chips, y_chip)
    y_outs.start()
    if nz // 2 > 4:
        ring_i.both(4)

    rowsums = jnp.zeros((TOK, TOK), F32)
    colsums, ends, maps = [], [], []
    for p in range(2):
        pair_sum = jnp.zeros((TOK, TOK), F32)
        for i in range(HALF):
            q = p * HALF + i
            span = slice(i * HEAD, (i + 1) * HEAD)
            cross = dot(g[p, :, span], xtb[p, span, :])
            weights = dec[q] * cross
            pair_sum = pair_sum + weights * steps[q : q + 1, :]
            both = weights * inter[p]
            colsums.append(jnp.sum(both, axis=0, keepdims=True))
            row = jnp.sum(both * steps[q : q + 1, :], axis=1, keepdims=True)
            rowsums = jnp.where(ids1 == q, jnp.broadcast_to(row, (TOK, TOK)), rowsums)
            ends.append(
                jnp.sum(xtb[p, span, :].astype(F32) * abt[p, span, :], axis=0, keepdims=True)
            )
        maps.append(dot2(pair_sum, bs[p]))
        if nz // 2 > 5 + p:
            ring_i.both(5 + p)
    rowsums = rowsums.T[0 : 2 * HALF]

    state_back.recv()
    early = state_in[...].reshape(CH, STATE)
    state_at = [early, decay_rows[0] * early + s_first[...]]
    starts, corners = [], []
    for p in range(2):
        at_c = dot2(state_at[p], cs[p], NT)
        gs = gte[p]
        maps[p] = maps[p] + dot2(gs.T, state_at[p].astype(BF16))
        meets = adjoint_at[p] * state_at[p]
        for i in range(HALF):
            span = slice(i * HEAD, (i + 1) * HEAD)
            starts.append(jnp.sum(gs[span] * at_c[span], axis=0, keepdims=True))
            lanes = jnp.sum(meets[span], axis=0, keepdims=True)
            corners.append(
                jnp.broadcast_to(jnp.sum(lanes, axis=1, keepdims=True), (1, TOK))
            )
        m_own[p] = maps[p].reshape(2, TOK // 2, STATE)

    def map_to(j, s):
        rr, cc = (r + j // 2) % 2, (core + j % 2) % 2
        return remote(m_own.at[rr, cc], m_in.at[j], s, z * 2 + rr, 2 * k + cc)

    map_parts = Family("map_parts", 1, 4, map_to)
    map_parts.start()

    for n, parts in enumerate((colsums, ends, starts, corners)):
        for q in range(2 * HALF):
            vecs[2 + n, q : q + 1, :] = parts[q]
    colsum, end, start, corner = vecs[2], vecs[3], vecs[4], vecs[5]
    input_term = colsum + end_decay * end
    onward = (ids0 >= ids1).astype(F32)
    before = (ids0 < ids1).astype(F32)
    decay_term = (
        dot_exact(rowsums + start - steps * colsum, onward)
        + dot_exact(end_weight * end, before)
        + block_decay * corner
    )
    sigmoid = 1.0 / (1.0 + jnp.exp(-raw8))
    grads = sigmoid * (input_term + rates * decay_term)
    s_out[0, 0:HALF, :] = grads[0:HALF]
    s_out[0, HALF : 2 * HALF, :] = grads[0:HALF]
    s_out[1, 0:HALF, :] = grads[HALF : 2 * HALF]
    s_out[1, HALF : 2 * HALF, :] = grads[HALF : 2 * HALF]
    swap_s = remote(s_out.at[1 - r], s_swap, slot("s", 1), partner, c)
    swap_s.start()

    if nz // 2 > 7:
        ring_i.both(7)
    tcols.recv()
    each(1, chips, tcols_on.start_one)
    map_parts.recv()
    m_groups[k, core] = (m_own[r, core] + m_in[1] + m_in[2] + m_in[3]).astype(BF16)

    def map_out(j, s):
        at = m_groups.at[k, core]
        return remote(at, at, s, tok, xor(k, j, nk) * 2 + core)

    def map_on(j, s):
        at = m_groups.at[xor(k, j, nk), core]
        return remote(at, at, s, tok, sibling)

    map_outs = Family("map_out", 1, nk, map_out)
    map_ons = Family("map_on", 0, nk, map_on)
    map_outs.start()
    map_ons.start_one(0)
    ring_i.both(nz // 2)

    y_outs.recv()
    token_grad[...] = lax.fori_loop(
        0, chips, lambda j, total: total + y_in[j].astype(F32), jnp.zeros((TOK, CH), F32)
    ).astype(BF16)

    tcols_on.recv()

    def gather_term(n, totals):
        grad = ig[n]
        out = []
        for half in range(2):
            total = totals[half]
            for p in range(2):
                cols = tcol[p, :, half, n].reshape(TOK, TOK)
                total = total + dot(grad[p], cols)
            out.append(total)
        return tuple(out)

    zero = jnp.zeros((CH, TOK), F32)
    totals = lax.fori_loop(0, nz, gather_term, (zero, zero))
    for half in range(2):
        wgrad[half] = totals[half].T.astype(BF16)
    swap_o = remote(wgrad.at[1 - r], weight_grad.at[:, mine], slot("o", 1), partner, c)
    swap_o.start()
    weight_grad[:, mine] = wgrad[r]

    map_outs.recv()
    each(1, nk, map_ons.start_one)
    swap_s.wait_recv()
    own = jnp.where(low_half, s_out[0], s_out[1])
    sub = lax.broadcasted_iota(jnp.int32, (2 * HALF, TOK), 0)
    step_grad[...] = jnp.where((sub < HALF) == low_half, own, s_swap[...])
    map_ons.recv()
    for gg in range(nk):
        map_grad[gg] = m_groups[gg].reshape(TOK, STATE).astype(F32)
    swap_o.wait_recv()

    for swap in (swap_r, swap_g, swap_c, swap_b, swap_w, swap_s, swap_o):
        swap.wait_send()
    ring_w.sent()
    ring_i.sent()
    for family in (
        feats,
        feats_on,
        decays,
        adj_out,
        adj_back,
        state_out,
        state_back,
        columns_out,
        tcols,
        tcols_on,
        y_sibs,
        y_outs,
        map_parts,
        map_outs,
        map_ons,
    ):
        family.sent()


def local(tokens, w, cot, b, c, raw, rate_log, skip):
    nz = lax.axis_size("tok") // 2
    nk = lax.axis_size("ch") // 2
    piece, rowt, chips = CH // nz, TOK // nk, 2 * nk
    sems = 7 + 8 * (nz // 2 + 1) + 6 * nz + 6 * chips + 4 + 3 * nk
    vmem = pl.BlockSpec(memory_space=pltpu.VMEM)
    smem = pl.BlockSpec(memory_space=pltpu.SMEM)
    v = pltpu.VMEM

    def body(*refs):
        kernel(nz, nk, *refs)

    return pl.pallas_call(
        body,
        out_shape=(
            jax.ShapeDtypeStruct((TOK, CH), BF16),
            jax.ShapeDtypeStruct((TOK, 2 * CH), BF16),
            jax.ShapeDtypeStruct((2 * HALF, TOK), F32),
            jax.ShapeDtypeStruct((nk, TOK, STATE), F32),
        ),
        in_specs=[vmem] * 6 + [smem] * 2,
        out_specs=(vmem,) * 4,
        scratch_shapes=[
            v((2 * nk, 2, TOK, CH), BF16),
            v((nz, 2, TOK, CH), BF16),
            v((nz, 2, CH, TOK), BF16),
            v((2, nk, 2, nz, rowt, TOK), BF16),
            v((2, TOK, CH), BF16),
            v((2, TOK, STATE), BF16),
            v((2, TOK, STATE), BF16),
            v((2, 2 * HALF, TOK), F32),
            v((2 * HALF, TOK), F32),
            v((nz, 2 * HALF, TOK), F32),
            v((2, nz, piece, STATE), BF16),
            v((2, nz, piece, STATE), BF16),
            v((2, nz, piece, STATE), F32),
            v((nz, piece, STATE), F32),
            v((nz, piece, STATE), F32),
            v((2, CH, TOK), F32),
            v((2, CH, TOK), BF16),
            v((2, CH, TOK), BF16),
            v((2 * HALF, TOK, TOK), F32),
            v((2, TOK, TOK), F32),
            v((2, CH, TOK), F32),
            v((2, CH, TOK), F32),
            v((CH, STATE), F32),
            v((CH, STATE), F32),
            v((6, 2 * HALF, TOK), F32),
            v((2 * TOK, CH), BF16),
            v((2, nk, 2, TOK, CH), BF16),
            v((nk, 2, TOK, CH), BF16),
            v((nk, 2, TOK, CH), BF16),
            v((chips, TOK, CH), BF16),
            v((2, 2, TOK // 2, STATE), F32),
            v((4, TOK // 2, STATE), F32),
            v((nk, 2, TOK // 2, STATE), BF16),
            v((2, 2 * HALF, TOK), F32),
            v((2 * HALF, TOK), F32),
            v((2, TOK, CH), BF16),
            pltpu.SemaphoreType.DMA((1,)),
            pltpu.SemaphoreType.DMA((sems,)),
            pltpu.SemaphoreType.DMA((sems,)),
        ],
        compiler_params=pltpu.CompilerParams(
            collective_id=0, has_side_effects=True, vmem_limit_bytes=48 * 1024 * 1024
        ),
        name="mixer_backward",
    )(tokens, w, cot, b, c, raw, rate_log.reshape(1, 2 * HALF), skip.reshape(1, 2 * HALF))


def solution(mesh):
    return jax.shard_map(
        local,
        mesh=mesh,
        in_specs=(
            P("tok", "ch"),
            P("tok", "ch"),
            P("tok", "ch"),
            P(None, "tok", None),
            P(None, "tok", None),
            P("ch", "tok"),
            P("ch"),
            P("ch"),
        ),
        out_specs=(P("tok", "ch"), P("tok", "ch"), P("ch", "tok"), P(None, "tok", None)),
        check_vma=False,
    )
```

```python
import jax
import jax.numpy as jnp
from jax import lax
from jax.experimental import pallas as pl
from jax.experimental.pallas import tpu as pltpu
from jax.sharding import PartitionSpec as P

MESH = pl.DeviceIdType.MESH
HIGHEST = lax.Precision.HIGHEST
F32 = jnp.float32
BF16 = jnp.bfloat16
TOK = 128
HEAD = 64
HALF = 4
CH = HALF * HEAD
STATE = 128

NN = (((1,), (0,)), ((), ()))
NT = (((1,), (1,)), ((), ()))


def dot(a, b, dims=NN):
    return lax.dot_general(a, b, dims, preferred_element_type=F32)


def dot2(a, b, dims=NN):
    high = a.astype(BF16)
    low = (a - high.astype(F32)).astype(BF16)
    return dot(high, b, dims) + dot(low, b, dims)


def dot_exact(a, b):
    return lax.dot_general(a, b, NN, precision=HIGHEST, preferred_element_type=F32)


def heads_to_rows(rows, p):
    return jnp.concatenate(
        [
            jnp.broadcast_to(rows[p * HALF + i : p * HALF + i + 1], (HEAD, rows.shape[1]))
            for i in range(HALF)
        ],
        axis=0,
    )


def kernel(
    nz,
    nk,
    tokens,
    w,
    cot,
    b_in,
    c_in,
    raw_in,
    rate_log,
    skip_in,
    token_grad,
    weight_grad,
    step_grad,
    map_grad,
    feat,
    wg,
    ig,
    tcol,
    w_other,
    cot_other,
    b_other,
    c_other,
    raw_own,
    g,
    bs,
    cs,
    raw,
    dtile,
    dall,
    send_state,
    recv_state,
    back_state,
    state_in,
    gte,
    gtb,
    xtb,
    dec,
    inter,
    back_local,
    abt,
    a_last,
    s_first,
    vecs,
    igtm,
    proj,
    wtot,
    y_all,
    y_sib,
    y_out,
    y_in,
    m_own,
    m_in,
    m_groups,
    s_out,
    s_swap,
    wgrad,
    local_sem,
    send_sem,
    recv_sem,
):
    tok, c = lax.axis_index("tok"), lax.axis_index("ch")
    z, r = tok // 2, tok % 2
    k, core = c // 2, c % 2
    piece = CH // nz
    rowt = TOK // nk
    chips = 2 * nk
    hops = nz // 2
    partner = z * 2 + 1 - r
    sibling = c + 1 - 2 * core
    across = lax.rem(k + nk // 2, nk)
    mine = pl.ds(pl.multiple_of(r * CH, CH), CH)
    other = pl.ds(pl.multiple_of((1 - r) * CH, CH), CH)

    def ztok(zz, rr):
        return lax.rem(zz + nz, nz) * 2 + rr

    def xor(a, b, n):
        out, bit = 0, 1
        while bit < n:
            pa, pb = (a // bit) % 2, (b // bit) % 2
            out = out + bit * ((pa + pb) % 2)
            bit *= 2
        return out

    def chip(j):
        return (r + j // nk) % 2, xor(k, j % nk, nk)

    sends, recvs = [0], [0]

    def take(counter, n=1):
        counter[0] += n
        return counter[0] - n

    def remote(src, dst, s, q, tok_to, ch_to):
        return pltpu.make_async_remote_copy(
            src_ref=src,
            dst_ref=dst,
            send_sem=send_sem.at[s],
            recv_sem=recv_sem.at[q],
            device_id=(tok_to, ch_to),
            device_id_type=MESH,
        )

    def single(src, dst, tok_to, ch_to):
        return remote(src, dst, take(sends), take(recvs), tok_to, ch_to)

    def each(first, last, f):
        def body(j, carry):
            f(j)
            return carry

        lax.fori_loop(first, last, body, 0)

    class Family:
        def __init__(self, first, last, make, whole):
            self.first, self.last, self.whole = first, last, whole
            self.s, self.q = take(sends), take(recvs)
            self.make = lambda j: remote(*make(j)[:2], self.s, self.q, *make(j)[2:])
            self.all = lambda: remote(whole, whole, self.s, self.q, tok, sibling)

        def start(self):
            each(self.first, self.last, lambda j: self.make(j).start())

        def start_one(self, j):
            self.make(j).start()

        def recv(self):
            self.all().wait_recv()

        def sent(self):
            self.all().wait_send()

    class Ring:
        def __init__(self, buf, first):
            self.buf, self.first = buf, first
            self.rows = buf.shape[2] // 2
            self.s, self.q = take(sends), take(recvs, 8 * (hops + 1))

        def copy(self, way, s, n):
            block = lax.rem(z - way * (s - 1) + 2 * nz, nz)
            side = lax.rem(self.first + n // 2, 2)
            at = self.buf.at[block, side, pl.ds((n % 2) * self.rows, self.rows)]
            q = self.q + (s * 2 + (0 if way == 1 else 1)) * 4 + n
            return remote(at, at, self.s, q, ztok(z + way, r), c)

        def has(self, way, s, n):
            if s < hops:
                return True
            return s == hops and (n < 2) == (way == 1)

        def begin(self, n):
            for way in (1, -1):
                self.copy(way, 1, n).start()

        def tick(self, s, n):
            for way in (1, -1):
                if self.has(way, s, n):
                    self.copy(way, s, n).wait_recv()
                    if self.has(way, s + 1, n):
                        self.copy(way, s + 1, n).start()

        def ticks(self, group):
            for s, n in group:
                self.tick(s, n)

        def sent(self):
            whole = self.buf.at[pl.ds(0, nz - 1)]
            remote(whole, whole, self.s, self.q, tok, sibling).wait_send()

    loads = [
        pltpu.make_async_copy(src, dst, local_sem.at[n])
        for n, (src, dst) in enumerate(
            (
                (raw_in, raw_own),
                (cot.at[:, other], cot_other),
                (c_in.at[across], c_other),
                (w.at[:, mine], wg.at[z, r]),
                (w.at[:, other], w_other),
                (b_in.at[across], b_other),
                (tokens, feat.at[c, r]),
                (cot.at[:, mine], g.at[r]),
                (c_in.at[k], cs.at[r]),
                (b_in.at[k], bs.at[r]),
            )
        )
    ]
    for load in loads:
        load.start()

    barrier = pltpu.get_barrier_semaphore()

    def greet(tok_to, ch_to):
        pl.semaphore_signal(barrier, inc=1, device_id=(tok_to, ch_to), device_id_type=MESH)

    def greet_chip(j):
        rr, kk = chip(j)
        greet(z * 2 + rr, kk * 2 + core)

    each(1, nz, lambda j: greet(ztok(z + j, r), c))
    each(1, chips, greet_chip)
    greet(tok, sibling)
    greet(partner, sibling)
    for load in loads:
        load.wait()
    pl.semaphore_wait(barrier, (nz - 1) + (chips - 1) + 2)

    ring_w = Ring(wg, r)
    swap_r = single(raw_own, raw.at[r], partner, c)
    swap_g = single(cot_other, g.at[r], partner, c)
    swap_c = single(c_other, cs.at[r], partner, across * 2 + core)
    swap_w = single(w_other, wg.at[z, r], partner, c)
    swap_b = single(b_other, bs.at[r], partner, across * 2 + core)
    swap_r.start()
    swap_g.start()
    swap_c.start()
    ring_w.begin(0)
    ring_w.begin(1)
    swap_w.start()
    swap_b.start()

    def feat_out(j):
        rr, kk = chip(j)
        at = feat.at[c, r]
        return at, at, z * 2 + rr, kk * 2 + core

    def feat_on(j):
        rr, kk = chip(j)
        at = feat.at[kk * 2 + core, rr]
        return at, at, tok, sibling

    feats = Family(1, chips, feat_out, feat.at[pl.ds(0, chips - 1), 0])
    feats_on = Family(0, chips, feat_on, feat.at[:, 0])
    feats.start()
    feats_on.start_one(0)
    raw[r] = raw_own[...]

    groups_w = []
    for t in range(1, hops + 3):
        group = [(t, 0), (t, 1)] if t <= hops else []
        groups_w.append(group + ([(t - 2, 2), (t - 2, 3)] if t > 2 else []))
    groups_w += [[]] * (10 - len(groups_w))
    groups_i = [[(s, n) for n in range(4)] for s in range(1, hops)]
    groups_i += [[]] * (7 - len(groups_i)) + [[(hops, n) for n in range(4)]]

    ring_w.ticks(groups_w[0])
    swap_r.wait_recv()

    low_half = r == 0
    rows = []
    for p in range(2):
        both = raw[p]
        rows.append(jnp.where(low_half, both[0:HALF], both[HALF : 2 * HALF]))
    raw8 = jnp.concatenate(rows, axis=0)
    steps = jnp.maximum(raw8, 0.0) + jnp.log1p(jnp.exp(-jnp.abs(raw8)))
    for i in range(HALF):
        rate = jnp.full((1, TOK), rate_log[0, r * HALF + i], F32)
        skip = jnp.full((1, TOK), skip_in[0, r * HALF + i], F32)
        for p in range(2):
            vecs[0, p * HALF + i : p * HALF + i + 1, :] = rate
            vecs[1, p * HALF + i : p * HALF + i + 1, :] = skip
    rates = -jnp.exp(vecs[0])
    skips = vecs[1]
    ids0 = lax.broadcasted_iota(jnp.int32, (TOK, TOK), 0)
    ids1 = lax.broadcasted_iota(jnp.int32, (TOK, TOK), 1)
    upto = (ids0 <= ids1).astype(F32)
    log_decay = dot_exact(steps * rates, upto)
    log_total = jnp.broadcast_to(log_decay[:, TOK - 1 : TOK], (2 * HALF, TOK))
    start_decay = jnp.exp(log_decay)
    end_decay = jnp.exp(log_total - log_decay)
    end_weight = end_decay * steps
    block_decay = jnp.exp(log_total)
    decay_rows = [heads_to_rows(block_decay, p) for p in range(2)]
    columns = jnp.concatenate([log_decay, jnp.zeros((TOK - 2 * HALF, TOK), F32)], axis=0).T
    dtile[...] = jnp.concatenate(
        [block_decay[0:HALF] * block_decay[HALF : 2 * HALF], jnp.zeros((HALF, TOK), F32)], axis=0
    )
    dall[z] = dtile[...]

    def decay_out(j):
        return dtile, dall.at[z], ztok(z + j, r), c

    decays = Family(1, nz, decay_out, dall.at[pl.ds(0, nz - 1)])
    decays.start()
    ring_w.ticks(groups_w[1])

    swap_g.wait_recv()
    swap_c.wait_recv()
    adjoint = []
    for p in range(2):
        gt = g[p].astype(F32).T
        gtb[p] = gt.astype(BF16)
        gte[p] = gt * heads_to_rows(start_decay, p)
        adjoint.append(dot2(gte[p], cs[p]))
    a_last[...] = adjoint[1]

    class Exchange:
        def __init__(self, n, reverse):
            self.n, self.reverse = n, reverse

            def out(j):
                to = lax.rem(z + j, nz)
                return send_state.at[n, to], recv_state.at[n, z], ztok(to, r), c

            def back(j):
                to = lax.rem(z + j, nz)
                return back_state.at[n, to], state_in.at[n, z], ztok(to, r), c

            self.out = Family(1, nz, out, recv_state.at[n, pl.ds(0, nz - 1)])
            self.back = Family(1, nz, back, state_in.at[n, pl.ds(0, nz - 1)])

        def start(self, whole):
            n = self.n
            send_state[n] = whole.astype(BF16).reshape(nz, piece, STATE)
            self.out.start()
            recv_state[n, z] = send_state[n, z]

        def prefix(self):
            n = self.n
            head = (z * piece) // HEAD
            self.out.recv()
            carry = jnp.zeros((piece, STATE), F32)
            for at in reversed(range(nz)) if self.reverse else range(nz):
                back_state[n, at] = carry.astype(BF16)
                carry = dall[at, pl.ds(head, 1), :] * carry + recv_state[n, at].astype(F32)
            self.back.start()
            state_in[n, z] = back_state[n, z]

        def result(self):
            self.back.recv()
            return state_in[self.n].astype(F32).reshape(CH, STATE)

    adjoints = Exchange(0, True)
    adjoints.start(adjoint[0] + decay_rows[0] * adjoint[1])
    swap_w.wait_recv()
    ring_w.begin(2)
    ring_w.begin(3)
    ring_w.ticks(groups_w[2])
    swap_b.wait_recv()

    lower = ids0 >= ids1

    def block_kernels(p, heads):
        if heads[0] == 0:
            inter[p] = dot(cs[p], bs[p], NT)
        for i in heads:
            q = p * HALF + i
            gap = columns[:, q : q + 1] - log_decay[q : q + 1, :]
            dec[q] = jnp.where(lower, jnp.exp(jnp.minimum(gap, 0.0)), 0.0)
            kern = (dec[q] * inter[p]).astype(BF16)
            back_local[p, i * HEAD : (i + 1) * HEAD, :] = dot(
                gtb[p, i * HEAD : (i + 1) * HEAD, :], kern
            )

    block_kernels(0, (0, 1))
    ring_w.ticks(groups_w[3][:2])
    decays.recv()
    adjoints.prefix()
    ring_w.ticks(groups_w[3][2:])
    block_kernels(0, (2, 3))
    ring_w.ticks(groups_w[4][:2])
    block_kernels(1, (0, 1))
    ring_w.ticks(groups_w[4][2:])
    block_kernels(1, (2, 3))
    ring_w.ticks(groups_w[5])

    late = adjoints.result()
    ring_i = Ring(ig, 0)
    adjoint_at = [decay_rows[1] * late + a_last[...], late]
    for p in range(2):
        abt[p] = dot2(adjoint_at[p], bs[p], NT)
        back = back_local[p] + heads_to_rows(end_decay, p) * abt[p]
        grad = heads_to_rows(skips, p) * gtb[p].astype(F32) + heads_to_rows(steps, p) * back
        grad_low = grad.astype(BF16)
        ig[z, p] = grad_low
        ring_i.begin(2 * p)
        ring_i.begin(2 * p + 1)
        igtm[p * TOK : (p + 1) * TOK, :] = grad_low.astype(F32).T.astype(BF16)
    ring_w.ticks(groups_w[6])
    feats.recv()
    each(1, chips, feats_on.start_one)
    ring_i.ticks(groups_i[0])
    ring_w.ticks(groups_w[7])
    feats_on.recv()

    own_rows = pl.ds(pl.multiple_of(k * rowt, rowt), rowt)
    own_lanes = pl.ds(pl.multiple_of(core * TOK, TOK), TOK)
    me = r * nk + k

    def column_out(j):
        to = lax.rem(z + j, nz)
        src = feat.at[to, r, own_rows, own_lanes]
        return src, tcol.at[me, core, z], ztok(to, r), c

    own_columns = pltpu.make_async_copy(
        feat.at[z, r, own_rows, own_lanes], tcol.at[me, core, z], local_sem.at[0]
    )
    columns_out = Family(1, nz, column_out, tcol.at[0, 0, pl.ds(0, nz - 1)])

    def project(first, last):
        total = proj[...] if first else jnp.zeros((2 * TOK, CH), F32)
        for d in range(first, last):
            for way in (1, -1) if 0 < d < hops else (1,):
                n = lax.rem(z + way * d + nz, nz)
                total = total + dot(feat[n].reshape(2 * TOK, CH), wg[n].reshape(CH, CH))
        proj[...] = total

    project(0, min(3, hops))
    if hops > 3:
        ring_w.ticks(groups_w[8][:1])
        project(3, 6)
    ring_w.ticks(groups_w[8][1:] if hops > 3 else groups_w[8])
    ring_i.ticks(groups_i[1][:2])
    ring_w.ticks(groups_w[9])
    project(min(6, hops), hops + 1)
    states = []
    for p in range(2):
        xt = proj[p * TOK : (p + 1) * TOK, :].astype(BF16).astype(F32).T
        xtb[p] = xt.astype(BF16)
        states.append(dot2(xt * heads_to_rows(end_weight, p), bs[p]))
    s_first[...] = states[0]
    scan = Exchange(1, False)
    scan.start(decay_rows[1] * states[0] + states[1])
    own_columns.start()
    columns_out.start()
    ring_i.ticks(groups_i[1][2:])

    def term(kk, side):
        n = kk * 2 + side
        out = dot(igtm[...], wg[n].reshape(CH, CH), NT)
        y_all[side, kk] = out.astype(BF16).reshape(2, TOK, CH)

    def y_to_sibling(j):
        return y_all.at[1 - core, j], y_sib.at[j], tok, sibling

    y_sibs = Family(0, nk, y_to_sibling, y_sib)

    def first_terms(j):
        term(j, 1 - core)
        y_sibs.start_one(j)

    each(0, nk // 2, first_terms)
    ring_i.ticks(groups_i[2][:2])
    each(nk // 2, nk, first_terms)
    ring_i.ticks(groups_i[2][2:])

    scan.prefix()
    own_columns.wait()
    columns_out.recv()

    def tcol_out(j):
        rr, kk = chip(j)
        at = tcol.at[me, core]
        return at, at, z * 2 + rr, kk * 2 + core

    def tcol_on(j):
        rr, kk = chip(j)
        at = tcol.at[rr * nk + kk, core]
        return at, at, tok, sibling

    tcols = Family(1, chips, tcol_out, tcol.at[pl.ds(0, chips - 1), 0])
    tcols_on = Family(0, chips, tcol_on, tcol.at[:, 0])
    tcols.start()
    tcols_on.start_one(0)
    ring_i.ticks(groups_i[3][:2])
    each(0, nk // 2, lambda j: term(j, core))
    ring_i.ticks(groups_i[3][2:])
    each(nk // 2, nk, lambda j: term(j, core))

    rowsums = jnp.zeros((TOK, TOK), F32)
    colsums, ends, maps = [], [], []

    def pairs(p, heads, pair_sum, rowsums):
        for i in heads:
            q = p * HALF + i
            span = slice(i * HEAD, (i + 1) * HEAD)
            cross = dot(g[p, :, span], xtb[p, span, :])
            weights = dec[q] * cross
            pair_sum = pair_sum + weights * steps[q : q + 1, :]
            both = weights * inter[p]
            colsums.append(jnp.sum(both, axis=0, keepdims=True))
            row = jnp.sum(both * steps[q : q + 1, :], axis=1, keepdims=True)
            rowsums = jnp.where(ids1 == q, jnp.broadcast_to(row, (TOK, TOK)), rowsums)
            ends.append(
                jnp.sum(xtb[p, span, :].astype(F32) * abt[p, span, :], axis=0, keepdims=True)
            )
        return pair_sum, rowsums

    for p in range(2):
        pair_sum = jnp.zeros((TOK, TOK), F32)
        pair_sum, rowsums = pairs(p, (0, 1), pair_sum, rowsums)
        ring_i.ticks(groups_i[4][2 * p : 2 * p + 2])
        pair_sum, rowsums = pairs(p, (2, 3), pair_sum, rowsums)
        maps.append(dot2(pair_sum, bs[p]))
    rowsums = rowsums.T[0 : 2 * HALF]

    early = scan.result()
    state_at = [early, decay_rows[0] * early + s_first[...]]
    starts, corners = [], []
    for p in range(2):
        at_c = dot2(state_at[p], cs[p], NT)
        gs = gte[p]
        maps[p] = maps[p] + dot2(gs.T, state_at[p].astype(BF16))
        meets = adjoint_at[p] * state_at[p]
        for i in range(HALF):
            span = slice(i * HEAD, (i + 1) * HEAD)
            starts.append(jnp.sum(gs[span] * at_c[span], axis=0, keepdims=True))
            lanes = jnp.sum(meets[span], axis=0, keepdims=True)
            corners.append(
                jnp.broadcast_to(jnp.sum(lanes, axis=1, keepdims=True), (1, TOK))
            )
        m_own[p] = maps[p].reshape(2, TOK // 2, STATE)

    def map_to(j):
        rr, cc = (r + j // 2) % 2, (core + j % 2) % 2
        return m_own.at[rr, cc], m_in.at[j], z * 2 + rr, 2 * k + cc

    map_parts = Family(1, 4, map_to, m_in.at[pl.ds(1, 3)])
    map_parts.start()
    ring_i.ticks(groups_i[5])

    def y_sum(j):
        y_out[j] = (y_all[core, j].astype(F32) + y_sib[j].astype(F32)).astype(BF16)

    y_sibs.recv()
    each(0, nk, y_sum)
    y_in[0] = y_out[k, r]

    def y_chip(j):
        rr, kk = chip(j)
        return y_out.at[kk, rr], y_in.at[j], z * 2 + rr, kk * 2 + core

    y_outs = Family(1, chips, y_chip, y_in.at[pl.ds(1, chips - 1)])
    y_outs.start()

    for n, parts in enumerate((colsums, ends, starts, corners)):
        for q in range(2 * HALF):
            vecs[2 + n, q : q + 1, :] = parts[q]
    colsum, end, start, corner = vecs[2], vecs[3], vecs[4], vecs[5]
    input_term = colsum + end_decay * end
    onward = (ids0 >= ids1).astype(F32)
    before = (ids0 < ids1).astype(F32)
    decay_term = (
        dot_exact(rowsums + start - steps * colsum, onward)
        + dot_exact(end_weight * end, before)
        + block_decay * corner
    )
    sigmoid = 1.0 / (1.0 + jnp.exp(-raw8))
    grads = sigmoid * (input_term + rates * decay_term)
    s_out[0, 0:HALF, :] = grads[0:HALF]
    s_out[0, HALF : 2 * HALF, :] = grads[0:HALF]
    s_out[1, 0:HALF, :] = grads[HALF : 2 * HALF]
    s_out[1, HALF : 2 * HALF, :] = grads[HALF : 2 * HALF]
    swap_s = single(s_out.at[1 - r], s_swap, partner, c)
    swap_s.start()

    map_parts.recv()
    m_groups[k, core] = (m_own[r, core] + m_in[1] + m_in[2] + m_in[3]).astype(BF16)

    def map_out(j):
        at = m_groups.at[k, core]
        return at, at, tok, xor(k, j, nk) * 2 + core

    def map_on(j):
        at = m_groups.at[xor(k, j, nk), core]
        return at, at, tok, sibling

    map_outs = Family(1, nk, map_out, m_groups.at[pl.ds(0, nk - 1), 0])
    map_ons = Family(0, nk, map_on, m_groups.at[:, 0])
    map_outs.start()
    map_ons.start_one(0)
    ring_i.ticks(groups_i[6][:2])
    tcols.recv()
    each(1, chips, tcols_on.start_one)
    ring_i.ticks(groups_i[6][2:])

    def gather(first, last):
        for half in range(2):
            total = wtot[half] if first else jnp.zeros((CH, TOK), F32)
            for d in range(first, last):
                for way in (1, -1) if 0 < d < hops else (1,):
                    n = lax.rem(z + way * d + nz, nz)
                    for p in range(2):
                        cols = tcol[p * nk : (p + 1) * nk, half, n].reshape(TOK, TOK)
                        total = total + dot(ig[n, p], cols)
            wtot[half] = total

    swap_s.wait_recv()
    own = jnp.where(low_half, s_out[0], s_out[1])
    sub = lax.broadcasted_iota(jnp.int32, (2 * HALF, TOK), 0)
    step_grad[...] = jnp.where((sub < HALF) == low_half, own, s_swap[...])
    map_outs.recv()
    each(1, nk, map_ons.start_one)
    tcols_on.recv()
    gather(0, hops)
    ring_i.ticks(groups_i[7])
    gather(hops, hops + 1)
    for half in range(2):
        wgrad[half] = wtot[half].T.astype(BF16)
    swap_o = single(wgrad.at[1 - r], weight_grad.at[:, mine], partner, c)
    swap_o.start()
    weight_grad[:, mine] = wgrad[r]

    y_outs.recv()
    total = y_in[0].astype(F32)
    for j in range(1, chips):
        total = total + y_in[j].astype(F32)
    token_grad[...] = total.astype(BF16)
    map_ons.recv()
    for gg in range(nk):
        map_grad[gg] = m_groups[gg].reshape(TOK, STATE).astype(F32)

    for swap in (swap_r, swap_g, swap_c, swap_b, swap_w, swap_s):
        swap.wait_send()
    ring_w.sent()
    ring_i.sent()
    for family in (
        feats,
        feats_on,
        decays,
        adjoints.out,
        adjoints.back,
        scan.out,
        scan.back,
        columns_out,
        tcols,
        tcols_on,
        y_sibs,
        y_outs,
        map_parts,
        map_outs,
        map_ons,
    ):
        family.sent()
    swap_o.wait_recv()
    swap_o.wait_send()


def local(tokens, w, cot, b, c, raw, rate_log, skip):
    nz = lax.axis_size("tok") // 2
    nk = lax.axis_size("ch") // 2
    piece, rowt, chips = CH // nz, TOK // nk, 2 * nk
    vmem = pl.BlockSpec(memory_space=pltpu.VMEM)
    smem = pl.BlockSpec(memory_space=pltpu.SMEM)
    hbm = pl.BlockSpec(memory_space=pl.ANY)
    v = pltpu.VMEM

    def body(*refs):
        kernel(nz, nk, *refs)

    return pl.pallas_call(
        body,
        out_shape=(
            jax.ShapeDtypeStruct((TOK, CH), BF16),
            jax.ShapeDtypeStruct((TOK, 2 * CH), BF16),
            jax.ShapeDtypeStruct((2 * HALF, TOK), F32),
            jax.ShapeDtypeStruct((nk, TOK, STATE), F32),
        ),
        in_specs=[hbm] * 6 + [smem] * 2,
        out_specs=(vmem,) * 4,
        scratch_shapes=[
            v((2 * nk, 2, TOK, CH), BF16),
            v((nz, 2, TOK, CH), BF16),
            v((nz, 2, CH, TOK), BF16),
            v((2 * nk, 2, nz, rowt, TOK), BF16),
            v((TOK, CH), BF16),
            v((TOK, CH), BF16),
            v((TOK, STATE), BF16),
            v((TOK, STATE), BF16),
            v((2 * HALF, TOK), F32),
            v((2, TOK, CH), BF16),
            v((2, TOK, STATE), BF16),
            v((2, TOK, STATE), BF16),
            v((2, 2 * HALF, TOK), F32),
            v((2 * HALF, TOK), F32),
            v((nz, 2 * HALF, TOK), F32),
            v((2, nz, piece, STATE), BF16),
            v((2, nz, piece, STATE), BF16),
            v((2, nz, piece, STATE), BF16),
            v((2, nz, piece, STATE), BF16),
            v((2, CH, TOK), F32),
            v((2, CH, TOK), BF16),
            v((2, CH, TOK), BF16),
            v((2 * HALF, TOK, TOK), F32),
            v((2, TOK, TOK), F32),
            v((2, CH, TOK), F32),
            v((2, CH, TOK), F32),
            v((CH, STATE), F32),
            v((CH, STATE), F32),
            v((6, 2 * HALF, TOK), F32),
            v((2 * TOK, CH), BF16),
            v((2 * TOK, CH), F32),
            v((2, CH, TOK), F32),
            v((2, nk, 2, TOK, CH), BF16),
            v((nk, 2, TOK, CH), BF16),
            v((nk, 2, TOK, CH), BF16),
            v((chips, TOK, CH), BF16),
            v((2, 2, TOK // 2, STATE), F32),
            v((4, TOK // 2, STATE), F32),
            v((nk, 2, TOK // 2, STATE), BF16),
            v((2, 2 * HALF, TOK), F32),
            v((2 * HALF, TOK), F32),
            v((2, TOK, CH), BF16),
            pltpu.SemaphoreType.DMA((10,)),
            pltpu.SemaphoreType.DMA((24,)),
            pltpu.SemaphoreType.DMA((22 + 16 * (nz // 2 + 1),)),
        ],
        compiler_params=pltpu.CompilerParams(
            collective_id=0, has_side_effects=True, vmem_limit_bytes=60 * 1024 * 1024
        ),
        name="mixer_backward",
    )(tokens, w, cot, b, c, raw, rate_log.reshape(1, 2 * HALF), skip.reshape(1, 2 * HALF))


def solution(mesh):
    return jax.shard_map(
        local,
        mesh=mesh,
        in_specs=(
            P("tok", "ch"),
            P("tok", "ch"),
            P("tok", "ch"),
            P(None, "tok", None),
            P(None, "tok", None),
            P("ch", "tok"),
            P("ch"),
            P("ch"),
        ),
        out_specs=(P("tok", "ch"), P("tok", "ch"), P("ch", "tok"), P(None, "tok", None)),
        check_vma=False,
    )
```

```python
import jax
import jax.numpy as jnp
from jax import lax
from jax.experimental import pallas as pl
from jax.experimental.pallas import tpu as pltpu
from jax.sharding import PartitionSpec as P

MESH = pl.DeviceIdType.MESH
HIGHEST = lax.Precision.HIGHEST
F32 = jnp.float32
BF16 = jnp.bfloat16
TOK = 128
HEAD = 64
HALF = 4
CH = HALF * HEAD
STATE = 128

NN = (((1,), (0,)), ((), ()))
NT = (((1,), (1,)), ((), ()))


def dot(a, b, dims=NN):
    return lax.dot_general(a, b, dims, preferred_element_type=F32)


def dot2(a, b, dims=NN):
    high = a.astype(BF16)
    low = (a - high.astype(F32)).astype(BF16)
    return dot(high, b, dims) + dot(low, b, dims)


def dot_exact(a, b):
    return lax.dot_general(a, b, NN, precision=HIGHEST, preferred_element_type=F32)


def heads_to_rows(rows, p):
    return jnp.concatenate(
        [
            jnp.broadcast_to(rows[p * HALF + i : p * HALF + i + 1], (HEAD, rows.shape[1]))
            for i in range(HALF)
        ],
        axis=0,
    )


def kernel(
    nz,
    nk,
    tokens,
    w,
    cot,
    b_in,
    c_in,
    raw_in,
    rate_log,
    skip_in,
    token_grad,
    weight_grad,
    step_grad,
    map_grad,
    feat,
    wg,
    ig,
    tcol,
    tpre,
    w_other,
    cot_other,
    b_other,
    c_other,
    raw_own,
    g,
    bs,
    cs,
    raw,
    dtile,
    dall,
    send_state,
    recv_state,
    back_state,
    state_in,
    gte,
    gtb,
    xtb,
    dec,
    inter,
    back_local,
    abt,
    a_last,
    s_first,
    vecs,
    igtm,
    proj,
    wtot,
    y_all,
    y_sib,
    y_out,
    y_in,
    m_own,
    m_in,
    m_groups,
    s_out,
    s_swap,
    wgrad,
    local_sem,
    send_sem,
    recv_sem,
):
    tok, c = lax.axis_index("tok"), lax.axis_index("ch")
    z, r = tok // 2, tok % 2
    k, core = c // 2, c % 2
    piece = CH // nz
    rowt = TOK // nk
    chips = 2 * nk
    hops = nz // 2
    partner = z * 2 + 1 - r
    sibling = c + 1 - 2 * core
    across = lax.rem(k + nk // 2, nk)
    mine = pl.ds(pl.multiple_of(r * CH, CH), CH)
    other = pl.ds(pl.multiple_of((1 - r) * CH, CH), CH)
    me = r * nk + k

    def piece_of(kk, side):
        return (
            pl.ds(pl.multiple_of(kk * rowt, rowt), rowt),
            pl.ds(pl.multiple_of(side * TOK, TOK), TOK),
        )

    def ztok(zz, rr):
        return lax.rem(zz + nz, nz) * 2 + rr

    def xor(a, b, n):
        out, bit = 0, 1
        while bit < n:
            pa, pb = (a // bit) % 2, (b // bit) % 2
            out = out + bit * ((pa + pb) % 2)
            bit *= 2
        return out

    def chip(j):
        return (r + j // nk) % 2, xor(k, j % nk, nk)

    sends, recvs = [0], [0]

    def take(counter, n=1):
        counter[0] += n
        return counter[0] - n

    def remote(src, dst, s, q, tok_to, ch_to):
        return pltpu.make_async_remote_copy(
            src_ref=src,
            dst_ref=dst,
            send_sem=send_sem.at[s],
            recv_sem=recv_sem.at[q],
            device_id=(tok_to, ch_to),
            device_id_type=MESH,
        )

    def single(src, dst, tok_to, ch_to):
        return remote(src, dst, take(sends), take(recvs), tok_to, ch_to)

    def each(first, last, f):
        def body(j, carry):
            f(j)
            return carry

        lax.fori_loop(first, last, body, 0)

    class Family:
        def __init__(self, first, last, make, whole):
            self.first, self.last, self.whole = first, last, whole
            self.s, self.q = take(sends), take(recvs)
            self.make = lambda j: remote(*make(j)[:2], self.s, self.q, *make(j)[2:])
            self.all = lambda: remote(whole, whole, self.s, self.q, tok, sibling)

        def start(self):
            each(self.first, self.last, lambda j: self.make(j).start())

        def start_one(self, j):
            self.make(j).start()

        def recv(self):
            self.all().wait_recv()

        def sent(self):
            self.all().wait_send()

    class Ring:
        def __init__(self, buf, first):
            self.buf, self.first = buf, first
            self.rows = buf.shape[2] // 2
            self.s, self.q = take(sends), take(recvs, 8 * (hops + 1))

        def copy(self, way, s, n):
            block = lax.rem(z - way * (s - 1) + 2 * nz, nz)
            side = lax.rem(self.first + n // 2, 2)
            at = self.buf.at[block, side, pl.ds((n % 2) * self.rows, self.rows)]
            q = self.q + (s * 2 + (0 if way == 1 else 1)) * 4 + n
            return remote(at, at, self.s, q, ztok(z + way, r), c)

        def has(self, way, s, n):
            if s < hops:
                return True
            return s == hops and (n < 2) == (way == 1)

        def begin(self, n):
            for way in (1, -1):
                self.copy(way, 1, n).start()

        def tick(self, s, n):
            for way in (1, -1):
                if self.has(way, s, n):
                    self.copy(way, s, n).wait_recv()
                    if self.has(way, s + 1, n):
                        self.copy(way, s + 1, n).start()

        def ticks(self, group):
            for s, n in group:
                self.tick(s, n)

        def sent(self):
            whole = self.buf.at[pl.ds(0, nz - 1)]
            remote(whole, whole, self.s, self.q, tok, sibling).wait_send()

    loads = [
        pltpu.make_async_copy(src, dst, local_sem.at[n])
        for n, (src, dst) in enumerate(
            (
                (raw_in, raw_own),
                (cot.at[:, other], cot_other),
                (c_in.at[across], c_other),
                (w.at[:, mine], wg.at[z, r]),
                (w.at[:, other], w_other),
                (b_in.at[across], b_other),
                (tokens, feat.at[c, r]),
                (cot.at[:, mine], g.at[r]),
                (c_in.at[k], cs.at[r]),
                (b_in.at[k], bs.at[r]),
                (tokens.at[piece_of(k, core)], tpre.at[c]),
            )
        )
    ]
    for load in loads:
        load.start()

    barrier = pltpu.get_barrier_semaphore()

    def greet(tok_to, ch_to):
        pl.semaphore_signal(barrier, inc=1, device_id=(tok_to, ch_to), device_id_type=MESH)

    def greet_chip(j):
        rr, kk = chip(j)
        greet(z * 2 + rr, kk * 2 + core)

    each(1, nz, lambda j: greet(ztok(z + j, r), c))
    each(1, chips, greet_chip)
    each(1, nk, lambda j: greet(tok, xor(k, j, nk) * 2 + 1 - core))
    greet(tok, sibling)
    greet(partner, sibling)
    for load in loads:
        load.wait()
    pl.semaphore_wait(barrier, (nz - 1) + (chips - 1) + (nk - 1) + 2)

    ring_w = Ring(wg, r)
    swap_r = single(raw_own, raw.at[r], partner, c)
    swap_g = single(cot_other, g.at[r], partner, c)
    swap_c = single(c_other, cs.at[r], partner, across * 2 + core)
    swap_w = single(w_other, wg.at[z, r], partner, c)
    swap_b = single(b_other, bs.at[r], partner, across * 2 + core)
    swap_r.start()
    swap_w.start()
    ring_w.begin(0)
    ring_w.begin(1)
    swap_c.start()
    swap_b.start()
    swap_g.start()

    def piece_out(j):
        to = xor(c, j, 2 * nk)
        return feat.at[(c, r) + piece_of(to // 2, to % 2)], tpre.at[c], tok, to

    pieces = Family(1, 2 * nk, piece_out, tpre.at[pl.ds(0, 2 * nk - 1)])
    pieces.start()

    def feat_out(j):
        rr, kk = chip(j)
        at = feat.at[c, r]
        return at, at, z * 2 + rr, kk * 2 + core

    def feat_on(j):
        rr, kk = chip(j)
        at = feat.at[kk * 2 + core, rr]
        return at, at, tok, sibling

    feats = Family(1, chips, feat_out, feat.at[pl.ds(0, chips - 1), 0])
    feats_on = Family(0, chips, feat_on, feat.at[:, 0])
    raw[r] = raw_own[...]

    groups_w = []
    for t in range(1, hops + 3):
        group = [(t, 0), (t, 1)] if t <= hops else []
        groups_w.append(group + ([(t - 2, 2), (t - 2, 3)] if t > 2 else []))
    groups_w += [[]] * (10 - len(groups_w))
    groups_i = [[(s, n) for n in range(4)] for s in range(1, hops)]
    groups_i += [[]] * (7 - len(groups_i)) + [[(hops, n) for n in range(4)]]

    ring_w.ticks(groups_w[0])
    swap_r.wait_recv()

    low_half = r == 0
    rows = []
    for p in range(2):
        both = raw[p]
        rows.append(jnp.where(low_half, both[0:HALF], both[HALF : 2 * HALF]))
    raw8 = jnp.concatenate(rows, axis=0)
    steps = jnp.maximum(raw8, 0.0) + jnp.log1p(jnp.exp(-jnp.abs(raw8)))
    for i in range(HALF):
        rate = jnp.full((1, TOK), rate_log[0, r * HALF + i], F32)
        skip = jnp.full((1, TOK), skip_in[0, r * HALF + i], F32)
        for p in range(2):
            vecs[0, p * HALF + i : p * HALF + i + 1, :] = rate
            vecs[1, p * HALF + i : p * HALF + i + 1, :] = skip
    rates = -jnp.exp(vecs[0])
    skips = vecs[1]
    ids0 = lax.broadcasted_iota(jnp.int32, (TOK, TOK), 0)
    ids1 = lax.broadcasted_iota(jnp.int32, (TOK, TOK), 1)
    upto = (ids0 <= ids1).astype(F32)
    log_decay = dot_exact(steps * rates, upto)
    log_total = jnp.broadcast_to(log_decay[:, TOK - 1 : TOK], (2 * HALF, TOK))
    start_decay = jnp.exp(log_decay)
    end_decay = jnp.exp(log_total - log_decay)
    end_weight = end_decay * steps
    block_decay = jnp.exp(log_total)
    decay_rows = [heads_to_rows(block_decay, p) for p in range(2)]
    columns = jnp.concatenate([log_decay, jnp.zeros((TOK - 2 * HALF, TOK), F32)], axis=0).T
    dtile[...] = jnp.concatenate(
        [block_decay[0:HALF] * block_decay[HALF : 2 * HALF], jnp.zeros((HALF, TOK), F32)], axis=0
    )
    dall[z] = dtile[...]

    def decay_out(j):
        return dtile, dall.at[z], ztok(z + j, r), c

    decays = Family(1, nz, decay_out, dall.at[pl.ds(0, nz - 1)])
    decays.start()
    ring_w.ticks(groups_w[1])
    swap_w.wait_recv()
    ring_w.begin(2)
    ring_w.begin(3)

    def column_out(j):
        to = lax.rem(z + j, nz)
        return tpre.at[to], tcol.at[me, core, z], ztok(to, r), c

    pieces.recv()
    columns_out = Family(1, nz, column_out, tcol.at[0, 0, pl.ds(0, nz - 1)])
    columns_out.start()
    tcol[me, core, z] = tpre[z]
    ring_w.ticks(groups_w[2])

    swap_g.wait_recv()
    swap_c.wait_recv()
    feats.start()
    feats_on.start_one(0)
    adjoint = []
    for p in range(2):
        gt = g[p].astype(F32).T
        gtb[p] = gt.astype(BF16)
        gte[p] = gt * heads_to_rows(start_decay, p)
        adjoint.append(dot2(gte[p], cs[p]))
    a_last[...] = adjoint[1]

    class Exchange:
        def __init__(self, n, reverse):
            self.n, self.reverse = n, reverse

            def out(j):
                to = lax.rem(z + j, nz)
                return send_state.at[n, to], recv_state.at[n, z], ztok(to, r), c

            def back(j):
                to = lax.rem(z + j, nz)
                return back_state.at[n, to], state_in.at[n, z], ztok(to, r), c

            self.out = Family(1, nz, out, recv_state.at[n, pl.ds(0, nz - 1)])
            self.back = Family(1, nz, back, state_in.at[n, pl.ds(0, nz - 1)])

        def start(self, whole):
            n = self.n
            send_state[n] = whole.astype(BF16).reshape(nz, piece, STATE)
            self.out.start()
            recv_state[n, z] = send_state[n, z]

        def prefix(self):
            n = self.n
            head = (z * piece) // HEAD
            self.out.recv()
            carry = jnp.zeros((piece, STATE), F32)
            for at in reversed(range(nz)) if self.reverse else range(nz):
                back_state[n, at] = carry.astype(BF16)
                carry = dall[at, pl.ds(head, 1), :] * carry + recv_state[n, at].astype(F32)
            self.back.start()
            state_in[n, z] = back_state[n, z]

        def result(self):
            self.back.recv()
            return state_in[self.n].astype(F32).reshape(CH, STATE)

    adjoints = Exchange(0, True)
    adjoints.start(adjoint[0] + decay_rows[0] * adjoint[1])
    ring_w.ticks(groups_w[3])
    swap_b.wait_recv()

    lower = ids0 >= ids1

    def block_kernels(p, heads):
        if heads[0] == 0:
            inter[p] = dot(cs[p], bs[p], NT)
        for i in heads:
            q = p * HALF + i
            gap = columns[:, q : q + 1] - log_decay[q : q + 1, :]
            dec[q] = jnp.where(lower, jnp.exp(jnp.minimum(gap, 0.0)), 0.0)
            kern = (dec[q] * inter[p]).astype(BF16)
            back_local[p, i * HEAD : (i + 1) * HEAD, :] = dot(
                gtb[p, i * HEAD : (i + 1) * HEAD, :], kern
            )

    block_kernels(0, (0, 1, 2, 3))
    ring_w.ticks(groups_w[4])
    block_kernels(1, (0, 1, 2, 3))
    ring_w.ticks(groups_w[5])
    decays.recv()
    adjoints.prefix()
    ring_w.ticks(groups_w[6])
    columns_out.recv()

    def tcol_out(j):
        rr, kk = chip(j)
        at = tcol.at[me, core]
        return at, at, z * 2 + rr, kk * 2 + core

    def tcol_on(j):
        rr, kk = chip(j)
        at = tcol.at[rr * nk + kk, core]
        return at, at, tok, sibling

    tcols = Family(1, chips, tcol_out, tcol.at[pl.ds(0, chips - 1), 0])
    tcols_on = Family(0, chips, tcol_on, tcol.at[:, 0])
    ring_w.ticks(groups_w[7])
    feats.recv()
    each(1, chips, feats_on.start_one)
    tcols.start()
    tcols_on.start_one(0)
    ring_w.ticks(groups_w[8])

    def project(first, last):
        total = proj[...] if first else jnp.zeros((2 * TOK, CH), F32)
        for d in range(first, last):
            for way in (1, -1) if 0 < d < hops else (1,):
                n = lax.rem(z + way * d + nz, nz)
                total = total + dot(feat[n].reshape(2 * TOK, CH), wg[n].reshape(CH, CH))
        proj[...] = total

    feats_on.recv()
    project(0, hops)

    late = adjoints.result()
    ring_i = Ring(ig, 0)
    adjoint_at = [decay_rows[1] * late + a_last[...], late]
    for p in range(2):
        abt[p] = dot2(adjoint_at[p], bs[p], NT)
        back = back_local[p] + heads_to_rows(end_decay, p) * abt[p]
        grad = heads_to_rows(skips, p) * gtb[p].astype(F32) + heads_to_rows(steps, p) * back
        grad_low = grad.astype(BF16)
        ig[z, p] = grad_low
        ring_i.begin(2 * p)
        ring_i.begin(2 * p + 1)
        igtm[p * TOK : (p + 1) * TOK, :] = grad_low.astype(F32).T.astype(BF16)
    ring_w.ticks(groups_w[9])
    project(hops, hops + 1)
    states = []
    for p in range(2):
        xt = proj[p * TOK : (p + 1) * TOK, :].astype(BF16).astype(F32).T
        xtb[p] = xt.astype(BF16)
        states.append(dot2(xt * heads_to_rows(end_weight, p), bs[p]))
    s_first[...] = states[0]
    scan = Exchange(1, False)
    scan.start(decay_rows[1] * states[0] + states[1])
    ring_i.ticks(groups_i[0][:2])

    def term(kk, side):
        n = kk * 2 + side
        out = dot(igtm[...], wg[n].reshape(CH, CH), NT)
        y_all[side, kk] = out.astype(BF16).reshape(2, TOK, CH)

    def y_to_sibling(j):
        return y_all.at[1 - core, j], y_sib.at[j], tok, sibling

    y_sibs = Family(0, nk, y_to_sibling, y_sib)

    def first_terms(j):
        term(j, 1 - core)
        y_sibs.start_one(j)

    each(0, nk // 2, first_terms)
    ring_i.ticks(groups_i[0][2:])
    each(nk // 2, nk, first_terms)
    ring_i.ticks(groups_i[1][:2])
    each(0, nk // 2, lambda j: term(j, core))
    ring_i.ticks(groups_i[1][2:])
    each(nk // 2, nk, lambda j: term(j, core))
    y_sibs.recv()

    def y_sum(j):
        y_out[j] = (y_all[core, j].astype(F32) + y_sib[j].astype(F32)).astype(BF16)

    each(0, nk, y_sum)
    y_in[0] = y_out[k, r]

    def y_chip(j):
        rr, kk = chip(j)
        return y_out.at[kk, rr], y_in.at[j], z * 2 + rr, kk * 2 + core

    y_outs = Family(1, chips, y_chip, y_in.at[pl.ds(1, chips - 1)])
    y_outs.start()
    ring_i.ticks(groups_i[2])

    rowsums = jnp.zeros((TOK, TOK), F32)
    colsums, ends, maps = [], [], []

    def pairs(p, heads, pair_sum, rowsums):
        for i in heads:
            q = p * HALF + i
            span = slice(i * HEAD, (i + 1) * HEAD)
            cross = dot(g[p, :, span], xtb[p, span, :])
            weights = dec[q] * cross
            pair_sum = pair_sum + weights * steps[q : q + 1, :]
            both = weights * inter[p]
            colsums.append(jnp.sum(both, axis=0, keepdims=True))
            row = jnp.sum(both * steps[q : q + 1, :], axis=1, keepdims=True)
            rowsums = jnp.where(ids1 == q, jnp.broadcast_to(row, (TOK, TOK)), rowsums)
            ends.append(
                jnp.sum(xtb[p, span, :].astype(F32) * abt[p, span, :], axis=0, keepdims=True)
            )
        return pair_sum, rowsums

    for p in range(2):
        pair_sum = jnp.zeros((TOK, TOK), F32)
        pair_sum, rowsums = pairs(p, (0, 1, 2, 3), pair_sum, rowsums)
        maps.append(dot2(pair_sum, bs[p]))
        ring_i.ticks(groups_i[3][2 * p : 2 * p + 2])
    rowsums = rowsums.T[0 : 2 * HALF]
    scan.prefix()
    tcols.recv()
    each(1, chips, tcols_on.start_one)
    ring_i.ticks(groups_i[4])

    def gather(first, last):
        for half in range(2):
            total = wtot[half] if first else jnp.zeros((CH, TOK), F32)
            for d in range(first, last):
                for way in (1, -1) if 0 < d < hops else (1,):
                    n = lax.rem(z + way * d + nz, nz)
                    for p in range(2):
                        cols = tcol[p * nk : (p + 1) * nk, half, n].reshape(TOK, TOK)
                        total = total + dot(ig[n, p], cols)
            wtot[half] = total

    tcols_on.recv()
    gather(0, min(4, hops))
    ring_i.ticks(groups_i[5])
    gather(min(4, hops), min(6, hops))
    ring_i.ticks(groups_i[6])
    gather(min(6, hops), hops)

    early = scan.result()
    state_at = [early, decay_rows[0] * early + s_first[...]]
    starts, corners = [], []
    for p in range(2):
        at_c = dot2(state_at[p], cs[p], NT)
        gs = gte[p]
        maps[p] = maps[p] + dot2(gs.T, state_at[p].astype(BF16))
        meets = adjoint_at[p] * state_at[p]
        for i in range(HALF):
            span = slice(i * HEAD, (i + 1) * HEAD)
            starts.append(jnp.sum(gs[span] * at_c[span], axis=0, keepdims=True))
            lanes = jnp.sum(meets[span], axis=0, keepdims=True)
            corners.append(
                jnp.broadcast_to(jnp.sum(lanes, axis=1, keepdims=True), (1, TOK))
            )
        m_own[p] = maps[p].reshape(2, TOK // 2, STATE)

    def map_to(j):
        rr, cc = (r + j // 2) % 2, (core + j % 2) % 2
        return m_own.at[rr, cc], m_in.at[j], z * 2 + rr, 2 * k + cc

    map_parts = Family(1, 4, map_to, m_in.at[pl.ds(1, 3)])
    map_parts.start()
    ring_i.ticks(groups_i[7])
    gather(hops, hops + 1)
    for half in range(2):
        wgrad[half] = wtot[half].T.astype(BF16)
    swap_o = single(wgrad.at[1 - r], weight_grad.at[:, mine], partner, c)
    swap_o.start()
    weight_grad[:, mine] = wgrad[r]

    for n, parts in enumerate((colsums, ends, starts, corners)):
        for q in range(2 * HALF):
            vecs[2 + n, q : q + 1, :] = parts[q]
    colsum, end, start, corner = vecs[2], vecs[3], vecs[4], vecs[5]
    input_term = colsum + end_decay * end
    onward = (ids0 >= ids1).astype(F32)
    before = (ids0 < ids1).astype(F32)
    decay_term = (
        dot_exact(rowsums + start - steps * colsum, onward)
        + dot_exact(end_weight * end, before)
        + block_decay * corner
    )
    sigmoid = 1.0 / (1.0 + jnp.exp(-raw8))
    grads = sigmoid * (input_term + rates * decay_term)
    s_out[0, 0:HALF, :] = grads[0:HALF]
    s_out[0, HALF : 2 * HALF, :] = grads[0:HALF]
    s_out[1, 0:HALF, :] = grads[HALF : 2 * HALF]
    s_out[1, HALF : 2 * HALF, :] = grads[HALF : 2 * HALF]
    swap_s = single(s_out.at[1 - r], s_swap, partner, c)
    swap_s.start()

    map_parts.recv()
    m_groups[c] = (m_own[r, core] + m_in[1] + m_in[2] + m_in[3]).astype(BF16)

    def map_out(j):
        return m_groups.at[c], m_groups.at[c], tok, xor(c, j, 2 * nk)

    map_outs = Family(1, 2 * nk, map_out, m_groups.at[pl.ds(0, 2 * nk - 1)])
    map_outs.start()

    y_outs.recv()
    total = y_in[0].astype(F32)
    for j in range(1, chips):
        total = total + y_in[j].astype(F32)
    token_grad[...] = total.astype(BF16)
    swap_s.wait_recv()
    own = jnp.where(low_half, s_out[0], s_out[1])
    sub = lax.broadcasted_iota(jnp.int32, (2 * HALF, TOK), 0)
    step_grad[...] = jnp.where((sub < HALF) == low_half, own, s_swap[...])
    map_outs.recv()
    for n in range(2 * nk):
        rows = slice((n % 2) * (TOK // 2), (n % 2 + 1) * (TOK // 2))
        map_grad[n // 2, rows, :] = m_groups[n].astype(F32)

    for swap in (swap_r, swap_g, swap_c, swap_b, swap_w, swap_s):
        swap.wait_send()
    ring_w.sent()
    ring_i.sent()
    for family in (
        feats,
        feats_on,
        decays,
        adjoints.out,
        adjoints.back,
        scan.out,
        scan.back,
        columns_out,
        tcols,
        tcols_on,
        y_sibs,
        y_outs,
        map_parts,
        map_outs,
        pieces,
    ):
        family.sent()
    swap_o.wait_recv()
    swap_o.wait_send()


def local(tokens, w, cot, b, c, raw, rate_log, skip):
    nz = lax.axis_size("tok") // 2
    nk = lax.axis_size("ch") // 2
    piece, rowt, chips = CH // nz, TOK // nk, 2 * nk
    vmem = pl.BlockSpec(memory_space=pltpu.VMEM)
    smem = pl.BlockSpec(memory_space=pltpu.SMEM)
    hbm = pl.BlockSpec(memory_space=pl.ANY)
    v = pltpu.VMEM

    def body(*refs):
        kernel(nz, nk, *refs)

    return pl.pallas_call(
        body,
        out_shape=(
            jax.ShapeDtypeStruct((TOK, CH), BF16),
            jax.ShapeDtypeStruct((TOK, 2 * CH), BF16),
            jax.ShapeDtypeStruct((2 * HALF, TOK), F32),
            jax.ShapeDtypeStruct((nk, TOK, STATE), F32),
        ),
        in_specs=[hbm] * 6 + [smem] * 2,
        out_specs=(vmem,) * 4,
        scratch_shapes=[
            v((2 * nk, 2, TOK, CH), BF16),
            v((nz, 2, TOK, CH), BF16),
            v((nz, 2, CH, TOK), BF16),
            v((2 * nk, 2, nz, rowt, TOK), BF16),
            v((2 * nk, rowt, TOK), BF16),
            v((TOK, CH), BF16),
            v((TOK, CH), BF16),
            v((TOK, STATE), BF16),
            v((TOK, STATE), BF16),
            v((2 * HALF, TOK), F32),
            v((2, TOK, CH), BF16),
            v((2, TOK, STATE), BF16),
            v((2, TOK, STATE), BF16),
            v((2, 2 * HALF, TOK), F32),
            v((2 * HALF, TOK), F32),
            v((nz, 2 * HALF, TOK), F32),
            v((2, nz, piece, STATE), BF16),
            v((2, nz, piece, STATE), BF16),
            v((2, nz, piece, STATE), BF16),
            v((2, nz, piece, STATE), BF16),
            v((2, CH, TOK), F32),
            v((2, CH, TOK), BF16),
            v((2, CH, TOK), BF16),
            v((2 * HALF, TOK, TOK), F32),
            v((2, TOK, TOK), F32),
            v((2, CH, TOK), F32),
            v((2, CH, TOK), F32),
            v((CH, STATE), F32),
            v((CH, STATE), F32),
            v((6, 2 * HALF, TOK), F32),
            v((2 * TOK, CH), BF16),
            v((2 * TOK, CH), F32),
            v((2, CH, TOK), F32),
            v((2, nk, 2, TOK, CH), BF16),
            v((nk, 2, TOK, CH), BF16),
            v((nk, 2, TOK, CH), BF16),
            v((chips, TOK, CH), BF16),
            v((2, 2, TOK // 2, STATE), F32),
            v((4, TOK // 2, STATE), F32),
            v((2 * nk, TOK // 2, STATE), BF16),
            v((2, 2 * HALF, TOK), F32),
            v((2 * HALF, TOK), F32),
            v((2, TOK, CH), BF16),
            pltpu.SemaphoreType.DMA((11,)),
            pltpu.SemaphoreType.DMA((24,)),
            pltpu.SemaphoreType.DMA((22 + 16 * (nz // 2 + 1),)),
        ],
        compiler_params=pltpu.CompilerParams(
            collective_id=0, has_side_effects=True, vmem_limit_bytes=60 * 1024 * 1024
        ),
        name="mixer_backward",
    )(tokens, w, cot, b, c, raw, rate_log.reshape(1, 2 * HALF), skip.reshape(1, 2 * HALF))


def solution(mesh):
    return jax.shard_map(
        local,
        mesh=mesh,
        in_specs=(
            P("tok", "ch"),
            P("tok", "ch"),
            P("tok", "ch"),
            P(None, "tok", None),
            P(None, "tok", None),
            P("ch", "tok"),
            P("ch"),
            P("ch"),
        ),
        out_specs=(P("tok", "ch"), P("tok", "ch"), P("ch", "tok"), P(None, "tok", None)),
        check_vma=False,
    )
```

```python
import jax
import jax.numpy as jnp
from jax import lax
from jax.experimental import pallas as pl
from jax.experimental.pallas import tpu as pltpu
from jax.sharding import PartitionSpec as P

MESH = pl.DeviceIdType.MESH
HIGHEST = lax.Precision.HIGHEST
F32 = jnp.float32
BF16 = jnp.bfloat16
TOK = 128
HEAD = 64
HALF = 4
CH = HALF * HEAD
STATE = 128

NN = (((1,), (0,)), ((), ()))
NT = (((1,), (1,)), ((), ()))


def dot(a, b, dims=NN):
    return lax.dot_general(a, b, dims, preferred_element_type=F32)


def dot2(a, b, dims=NN):
    high = a.astype(BF16)
    low = (a - high.astype(F32)).astype(BF16)
    return dot(high, b, dims) + dot(low, b, dims)


def dot_exact(a, b):
    return lax.dot_general(a, b, NN, precision=HIGHEST, preferred_element_type=F32)


def heads_to_rows(rows, p):
    return jnp.concatenate(
        [
            jnp.broadcast_to(rows[p * HALF + i : p * HALF + i + 1], (HEAD, rows.shape[1]))
            for i in range(HALF)
        ],
        axis=0,
    )


def kernel(
    nz,
    nk,
    tokens,
    w,
    cot,
    b_in,
    c_in,
    raw_in,
    rate_log,
    skip_in,
    token_grad,
    weight_grad,
    step_grad,
    map_grad,
    feat,
    wg,
    ig,
    tcol,
    tpre,
    w_other,
    cot_other,
    g_relay,
    b_other,
    c_other,
    raw_own,
    g,
    bs,
    cs,
    raw,
    dtile,
    dall,
    send_state,
    recv_state,
    back_state,
    state_in,
    gte,
    gtb,
    xtb,
    dec,
    inter,
    back_local,
    abt,
    a_last,
    s_first,
    vecs,
    igtm,
    proj,
    wtot,
    y_all,
    y_sib,
    y_out,
    y_in,
    m_own,
    m_in,
    m_groups,
    s_out,
    s_swap,
    wgrad,
    local_sem,
    send_sem,
    recv_sem,
):
    tok, c = lax.axis_index("tok"), lax.axis_index("ch")
    z, r = tok // 2, tok % 2
    k, core = c // 2, c % 2
    piece = CH // nz
    rowt = TOK // nk
    chips = 2 * nk
    hops = nz // 2
    partner = z * 2 + 1 - r
    sibling = c + 1 - 2 * core
    across = lax.rem(k + nk // 2, nk)
    low = k // (nk // 2)
    r_before = low * r + (1 - low) * (1 - r)
    r_after = low * (1 - r) + (1 - low) * r
    mine = pl.ds(pl.multiple_of(r * CH, CH), CH)
    other = pl.ds(pl.multiple_of((1 - r) * CH, CH), CH)
    me = r * nk + k

    def piece_of(kk, side):
        return (
            pl.ds(pl.multiple_of(kk * rowt, rowt), rowt),
            pl.ds(pl.multiple_of(side * TOK, TOK), TOK),
        )

    def ztok(zz, rr):
        return lax.rem(zz + nz, nz) * 2 + rr

    def xor(a, b, n):
        out, bit = 0, 1
        while bit < n:
            pa, pb = (a // bit) % 2, (b // bit) % 2
            out = out + bit * ((pa + pb) % 2)
            bit *= 2
        return out

    def chip(j):
        return (r + j // nk) % 2, xor(k, j % nk, nk)

    sends, recvs = [0], [0]

    def take(counter, n=1):
        counter[0] += n
        return counter[0] - n

    def remote(src, dst, s, q, tok_to, ch_to):
        return pltpu.make_async_remote_copy(
            src_ref=src,
            dst_ref=dst,
            send_sem=send_sem.at[s],
            recv_sem=recv_sem.at[q],
            device_id=(tok_to, ch_to),
            device_id_type=MESH,
        )

    def single(src, dst, tok_to, ch_to):
        return remote(src, dst, take(sends), take(recvs), tok_to, ch_to)

    def each(first, last, f):
        def body(j, carry):
            f(j)
            return carry

        lax.fori_loop(first, last, body, 0)

    class Family:
        def __init__(self, first, last, make, whole):
            self.first, self.last, self.whole = first, last, whole
            self.s, self.q = take(sends), take(recvs)
            self.make = lambda j: remote(*make(j)[:2], self.s, self.q, *make(j)[2:])
            self.all = lambda: remote(whole, whole, self.s, self.q, tok, sibling)

        def start(self):
            each(self.first, self.last, lambda j: self.make(j).start())

        def start_one(self, j):
            self.make(j).start()

        def recv(self):
            self.all().wait_recv()

        def sent(self):
            self.all().wait_send()

    class Ring:
        def __init__(self, buf, first):
            self.buf, self.first = buf, first
            self.rows = buf.shape[2] // 2
            self.s, self.q = take(sends), take(recvs, 8 * (hops + 1))

        def copy(self, way, s, n):
            block = lax.rem(z - way * (s - 1) + 2 * nz, nz)
            side = lax.rem(self.first + n // 2, 2)
            at = self.buf.at[block, side, pl.ds((n % 2) * self.rows, self.rows)]
            q = self.q + (s * 2 + (0 if way == 1 else 1)) * 4 + n
            return remote(at, at, self.s, q, ztok(z + way, r), c)

        def has(self, way, s, n):
            if s < hops:
                return True
            return s == hops and (n < 2) == (way == 1)

        def begin(self, n):
            for way in (1, -1):
                self.copy(way, 1, n).start()

        def tick(self, s, n):
            for way in (1, -1):
                if self.has(way, s, n):
                    self.copy(way, s, n).wait_recv()
                    if self.has(way, s + 1, n):
                        self.copy(way, s + 1, n).start()

        def ticks(self, group):
            for s, n in group:
                self.tick(s, n)

        def sent(self):
            whole = self.buf.at[pl.ds(0, nz - 1)]
            remote(whole, whole, self.s, self.q, tok, sibling).wait_send()

    loads = [
        pltpu.make_async_copy(src, dst, local_sem.at[n])
        for n, (src, dst) in enumerate(
            (
                (raw_in, raw_own),
                (cot.at[:, other], cot_other),
                (c_in.at[across], c_other),
                (w.at[:, mine], wg.at[z, r]),
                (w.at[:, other], w_other),
                (b_in.at[across], b_other),
                (tokens, feat.at[c, r]),
                (cot.at[:, mine], g.at[r]),
                (c_in.at[k], cs.at[r]),
                (b_in.at[k], bs.at[r]),
                (tokens.at[piece_of(k, core)], tpre.at[c]),
            )
        )
    ]
    for load in loads:
        load.start()

    barrier = pltpu.get_barrier_semaphore()

    def greet(tok_to, ch_to):
        pl.semaphore_signal(barrier, inc=1, device_id=(tok_to, ch_to), device_id_type=MESH)

    def greet_chip(j):
        rr, kk = chip(j)
        greet(z * 2 + rr, kk * 2 + core)

    each(1, nz, lambda j: greet(ztok(z + j, r), c))
    each(1, chips, greet_chip)
    each(1, nk, lambda j: greet(tok, xor(k, j, nk) * 2 + 1 - core))
    greet(tok, sibling)
    greet(partner, sibling)
    for load in loads:
        load.wait()
    pl.semaphore_wait(barrier, (nz - 1) + (chips - 1) + (nk - 1) + 2)

    ring_w = Ring(wg, r)
    swap_r = single(raw_own, raw.at[r], partner, c)
    swap_g = single(cot_other, g_relay, z * 2 + r_before, across * 2 + core)
    relay_g = single(g_relay, g.at[r_after], z * 2 + r_before, across * 2 + core)
    swap_c = single(c_other, cs.at[r], partner, across * 2 + core)
    swap_w = single(w_other, wg.at[z, r], partner, c)
    swap_b = single(b_other, bs.at[r], partner, across * 2 + core)
    swap_r.start()
    swap_g.start()
    swap_w.start()
    ring_w.begin(0)
    ring_w.begin(1)
    swap_c.start()
    swap_b.start()

    def piece_out(j):
        to = xor(c, j, 2 * nk)
        return feat.at[(c, r) + piece_of(to // 2, to % 2)], tpre.at[c], tok, to

    pieces = Family(1, 2 * nk, piece_out, tpre.at[pl.ds(0, 2 * nk - 1)])
    pieces.start()

    def feat_out(j):
        rr, kk = chip(j)
        at = feat.at[c, r]
        return at, at, z * 2 + rr, kk * 2 + core

    def feat_on(j):
        rr, kk = chip(j)
        at = feat.at[kk * 2 + core, rr]
        return at, at, tok, sibling

    feats = Family(1, chips, feat_out, feat.at[pl.ds(0, chips - 1), 0])
    feats_on = Family(0, chips, feat_on, feat.at[:, 0])
    raw[r] = raw_own[...]

    def own(t):
        if t <= hops:
            ring_w.ticks([(t, 0), (t, 1)])

    def far(t):
        if t <= hops:
            ring_w.ticks([(t, 2), (t, 3)])

    def grads(t):
        if t < hops or t == 8:
            ring_i.ticks([(min(t, hops), n) for n in range(4)])

    own(1)
    swap_r.wait_recv()

    low_half = r == 0
    rows = []
    for p in range(2):
        both = raw[p]
        rows.append(jnp.where(low_half, both[0:HALF], both[HALF : 2 * HALF]))
    raw8 = jnp.concatenate(rows, axis=0)
    steps = jnp.maximum(raw8, 0.0) + jnp.log1p(jnp.exp(-jnp.abs(raw8)))
    for i in range(HALF):
        rate = jnp.full((1, TOK), rate_log[0, r * HALF + i], F32)
        skip = jnp.full((1, TOK), skip_in[0, r * HALF + i], F32)
        for p in range(2):
            vecs[0, p * HALF + i : p * HALF + i + 1, :] = rate
            vecs[1, p * HALF + i : p * HALF + i + 1, :] = skip
    rates = -jnp.exp(vecs[0])
    skips = vecs[1]
    ids0 = lax.broadcasted_iota(jnp.int32, (TOK, TOK), 0)
    ids1 = lax.broadcasted_iota(jnp.int32, (TOK, TOK), 1)
    upto = (ids0 <= ids1).astype(F32)
    log_decay = dot_exact(steps * rates, upto)
    log_total = jnp.broadcast_to(log_decay[:, TOK - 1 : TOK], (2 * HALF, TOK))
    start_decay = jnp.exp(log_decay)
    end_decay = jnp.exp(log_total - log_decay)
    end_weight = end_decay * steps
    block_decay = jnp.exp(log_total)
    decay_rows = [heads_to_rows(block_decay, p) for p in range(2)]
    columns = jnp.concatenate([log_decay, jnp.zeros((TOK - 2 * HALF, TOK), F32)], axis=0).T
    lane = lax.broadcasted_iota(jnp.int32, (1, TOK), 1)
    decay_row = jnp.zeros((1, TOK), F32)
    for i in range(HALF):
        decay_row = jnp.where(
            lane == i, block_decay[i : i + 1] * block_decay[HALF + i : HALF + i + 1], decay_row
        )
    dtile[...] = decay_row
    dall[z] = decay_row

    def decay_out(j):
        return dtile, dall.at[z], ztok(z + j, r), c

    decays = Family(1, nz, decay_out, dall.at[pl.ds(0, nz - 1)])
    decays.start()
    swap_g.wait_recv()
    relay_g.start()
    own(2)
    relay_g.wait_recv()
    swap_c.wait_recv()
    adjoint = []
    for p in range(2):
        gt = g[p].astype(F32).T
        gtb[p] = gt.astype(BF16)
        gte[p] = gt * heads_to_rows(start_decay, p)
        adjoint.append(dot2(gte[p], cs[p]))
    a_last[...] = adjoint[1]

    class Exchange:
        def __init__(self, n, reverse):
            self.n, self.reverse = n, reverse

            def out(j):
                to = lax.rem(z + j, nz)
                return send_state.at[n, to], recv_state.at[n, z], ztok(to, r), c

            def back(j):
                to = lax.rem(z + j, nz)
                return back_state.at[n, to], state_in.at[n, z], ztok(to, r), c

            self.out = Family(1, nz, out, recv_state.at[n, pl.ds(0, nz - 1)])
            self.back = Family(1, nz, back, state_in.at[n, pl.ds(0, nz - 1)])

        def start(self, whole):
            n = self.n
            send_state[n] = whole.astype(BF16).reshape(nz, piece, STATE)
            self.out.start()
            recv_state[n, z] = send_state[n, z]

        def prefix(self):
            n = self.n
            head = (z * piece) // HEAD
            self.out.recv()
            carry = jnp.zeros((piece, STATE), F32)
            own = jnp.where(lane == head, dall[...].reshape(nz, TOK), 0.0)
            decay = jnp.broadcast_to(jnp.sum(own, axis=1, keepdims=True), (nz, STATE))
            for at in reversed(range(nz)) if self.reverse else range(nz):
                back_state[n, at] = carry.astype(BF16)
                carry = decay[at : at + 1] * carry + recv_state[n, at].astype(F32)
            self.back.start()
            state_in[n, z] = back_state[n, z]

        def result(self):
            self.back.recv()
            return state_in[self.n].astype(F32).reshape(CH, STATE)

    adjoints = Exchange(0, True)
    adjoints.start(adjoint[0] + decay_rows[0] * adjoint[1])
    swap_w.wait_recv()
    ring_w.begin(2)
    ring_w.begin(3)
    own(3)
    feats.start()
    feats_on.start_one(0)
    swap_b.wait_recv()

    lower = ids0 >= ids1

    def block_kernels(p, heads):
        if heads[0] == 0:
            inter[p] = dot(cs[p], bs[p], NT)
        for i in heads:
            q = p * HALF + i
            gap = columns[:, q : q + 1] - log_decay[q : q + 1, :]
            dec[q] = jnp.where(lower, jnp.exp(jnp.minimum(gap, 0.0)), 0.0)
            kern = (dec[q] * inter[p]).astype(BF16)
            back_local[p, i * HEAD : (i + 1) * HEAD, :] = dot(
                gtb[p, i * HEAD : (i + 1) * HEAD, :], kern
            )

    block_kernels(0, (0, 1, 2, 3))
    far(1)
    own(4)
    block_kernels(1, (0, 1, 2, 3))
    decays.recv()
    adjoints.prefix()
    far(2)
    own(5)

    def column_out(j):
        to = lax.rem(z + j, nz)
        return tpre.at[to], tcol.at[me, core, z], ztok(to, r), c

    pieces.recv()
    columns_out = Family(1, nz, column_out, tcol.at[0, 0, pl.ds(0, nz - 1)])
    columns_out.start()
    tcol[me, core, z] = tpre[z]
    far(3)
    own(6)
    far(4)
    own(7)

    def tcol_out(j):
        rr, kk = chip(j)
        at = tcol.at[me, core]
        return at, at, z * 2 + rr, kk * 2 + core

    def tcol_on(j):
        rr, kk = chip(j)
        at = tcol.at[rr * nk + kk, core]
        return at, at, tok, sibling

    tcols = Family(1, chips, tcol_out, tcol.at[pl.ds(0, chips - 1), 0])
    tcols_on = Family(0, chips, tcol_on, tcol.at[:, 0])
    def project(first, last):
        total = proj[...] if first else jnp.zeros((2 * TOK, CH), F32)
        for d in range(first, last):
            for way in (1, -1) if 0 < d < hops else (1,):
                n = lax.rem(z + way * d + nz, nz)
                total = total + dot(feat[n].reshape(2 * TOK, CH), wg[n].reshape(CH, CH))
        proj[...] = total

    late = adjoints.result()
    ring_i = Ring(ig, 0)
    adjoint_at = [decay_rows[1] * late + a_last[...], late]
    for p in range(2):
        abt[p] = dot2(adjoint_at[p], bs[p], NT)
        back = back_local[p] + heads_to_rows(end_decay, p) * abt[p]
        grad = heads_to_rows(skips, p) * gtb[p].astype(F32) + heads_to_rows(steps, p) * back
        grad_low = grad.astype(BF16)
        ig[z, p] = grad_low
        ring_i.begin(2 * p)
        ring_i.begin(2 * p + 1)
        igtm[p * TOK : (p + 1) * TOK, :] = grad_low.astype(F32).T.astype(BF16)
    far(5)
    own(8)
    feats.recv()
    each(1, chips, feats_on.start_one)
    columns_out.recv()
    tcols.start()
    tcols_on.start_one(0)
    far(6)
    grads(1)
    feats_on.recv()
    project(0, min(6, hops))
    far(7)
    grads(2)
    project(min(6, hops), min(7, hops))
    far(8)
    project(min(7, hops), hops + 1)
    states = []
    for p in range(2):
        xt = proj[p * TOK : (p + 1) * TOK, :].astype(BF16).astype(F32).T
        xtb[p] = xt.astype(BF16)
        states.append(dot2(xt * heads_to_rows(end_weight, p), bs[p]))
    s_first[...] = states[0]
    scan = Exchange(1, False)
    scan.start(decay_rows[1] * states[0] + states[1])
    grads(3)

    def term(kk, side):
        n = kk * 2 + side
        out = dot(igtm[...], wg[n].reshape(CH, CH), NT)
        y_all[side, kk] = out.astype(BF16).reshape(2, TOK, CH)

    def y_to_sibling(j):
        return y_all.at[1 - core, j], y_sib.at[j], tok, sibling

    y_sibs = Family(0, nk, y_to_sibling, y_sib)

    def first_terms(j):
        term(j, 1 - core)
        y_sibs.start_one(j)

    each(0, nk // 2, first_terms)
    each(nk // 2, nk, first_terms)
    grads(4)
    each(0, nk, lambda j: term(j, core))
    y_sibs.recv()

    def y_sum(j):
        y_out[j] = (y_all[core, j].astype(F32) + y_sib[j].astype(F32)).astype(BF16)

    each(0, nk, y_sum)
    y_in[0] = y_out[k, r]

    def y_chip(j):
        rr, kk = chip(j)
        return y_out.at[kk, rr], y_in.at[j], z * 2 + rr, kk * 2 + core

    y_outs = Family(1, chips, y_chip, y_in.at[pl.ds(1, chips - 1)])
    y_outs.start()
    grads(5)

    rowsums = jnp.zeros((TOK, TOK), F32)
    colsums, ends, maps = [], [], []

    def pairs(p, heads, pair_sum, rowsums):
        for i in heads:
            q = p * HALF + i
            span = slice(i * HEAD, (i + 1) * HEAD)
            cross = dot(g[p, :, span], xtb[p, span, :])
            weights = dec[q] * cross
            pair_sum = pair_sum + weights * steps[q : q + 1, :]
            both = weights * inter[p]
            colsums.append(jnp.sum(both, axis=0, keepdims=True))
            row = jnp.sum(both * steps[q : q + 1, :], axis=1, keepdims=True)
            rowsums = jnp.where(ids1 == q, jnp.broadcast_to(row, (TOK, TOK)), rowsums)
            ends.append(
                jnp.sum(xtb[p, span, :].astype(F32) * abt[p, span, :], axis=0, keepdims=True)
            )
        return pair_sum, rowsums

    for p in range(2):
        pair_sum = jnp.zeros((TOK, TOK), F32)
        pair_sum, rowsums = pairs(p, (0, 1, 2, 3), pair_sum, rowsums)
        maps.append(dot2(pair_sum, bs[p]))
        if p == 0:
            scan.prefix()
    rowsums = rowsums.T[0 : 2 * HALF]
    grads(6)
    tcols.recv()
    each(1, chips, tcols_on.start_one)

    def gather(first, last):
        total = wtot[...] if first else jnp.zeros((CH, 2 * TOK), F32)
        for d in range(first, last):
            for way in (1, -1) if 0 < d < hops else (1,):
                n = lax.rem(z + way * d + nz, nz)
                grad = jnp.concatenate([ig[n, 0], ig[n, 1]], axis=1)
                cols = [tcol[:, half, n].reshape(2 * TOK, TOK) for half in range(2)]
                total = total + dot(grad, jnp.concatenate(cols, axis=1))
        wtot[...] = total

    grads(7)
    tcols_on.recv()
    gather(0, hops)

    early = scan.result()
    state_at = [early, decay_rows[0] * early + s_first[...]]
    starts, corners = [], []
    for p in range(2):
        at_c = dot2(state_at[p], cs[p], NT)
        gs = gte[p]
        maps[p] = maps[p] + dot2(gs.T, state_at[p].astype(BF16))
        meets = adjoint_at[p] * state_at[p]
        for i in range(HALF):
            span = slice(i * HEAD, (i + 1) * HEAD)
            starts.append(jnp.sum(gs[span] * at_c[span], axis=0, keepdims=True))
            lanes = jnp.sum(meets[span], axis=0, keepdims=True)
            corners.append(
                jnp.broadcast_to(jnp.sum(lanes, axis=1, keepdims=True), (1, TOK))
            )
        m_own[p] = maps[p].reshape(2, TOK // 2, STATE)

    def map_to(j):
        rr, cc = (r + j // 2) % 2, (core + j % 2) % 2
        return m_own.at[rr, cc], m_in.at[j], z * 2 + rr, 2 * k + cc

    map_parts = Family(1, 4, map_to, m_in.at[pl.ds(1, 3)])
    map_parts.start()
    grads(8)
    gather(hops, hops + 1)
    for half in range(2):
        wgrad[half] = wtot[:, half * TOK : (half + 1) * TOK].T.astype(BF16)
    swap_o = single(wgrad.at[1 - r], weight_grad.at[:, mine], partner, c)
    swap_o.start()
    weight_grad[:, mine] = wgrad[r]

    for n, parts in enumerate((colsums, ends, starts, corners)):
        for q in range(2 * HALF):
            vecs[2 + n, q : q + 1, :] = parts[q]
    colsum, end, start, corner = vecs[2], vecs[3], vecs[4], vecs[5]
    input_term = colsum + end_decay * end
    onward = (ids0 >= ids1).astype(F32)
    before = (ids0 < ids1).astype(F32)
    decay_term = (
        dot_exact(rowsums + start - steps * colsum, onward)
        + dot_exact(end_weight * end, before)
        + block_decay * corner
    )
    sigmoid = 1.0 / (1.0 + jnp.exp(-raw8))
    grads = sigmoid * (input_term + rates * decay_term)
    s_out[0, 0:HALF, :] = grads[0:HALF]
    s_out[0, HALF : 2 * HALF, :] = grads[0:HALF]
    s_out[1, 0:HALF, :] = grads[HALF : 2 * HALF]
    s_out[1, HALF : 2 * HALF, :] = grads[HALF : 2 * HALF]
    swap_s = single(s_out.at[1 - r], s_swap, partner, c)
    swap_s.start()

    map_parts.recv()
    m_groups[c] = (m_own[r, core] + m_in[1] + m_in[2] + m_in[3]).astype(BF16)

    def map_out(j):
        return m_groups.at[c], m_groups.at[c], tok, xor(c, j, 2 * nk)

    map_outs = Family(1, 2 * nk, map_out, m_groups.at[pl.ds(0, 2 * nk - 1)])
    map_outs.start()

    y_outs.recv()
    total = y_in[0].astype(F32)
    for j in range(1, chips):
        total = total + y_in[j].astype(F32)
    token_grad[...] = total.astype(BF16)
    swap_s.wait_recv()
    kept = jnp.where(low_half, s_out[0], s_out[1])
    sub = lax.broadcasted_iota(jnp.int32, (2 * HALF, TOK), 0)
    step_grad[...] = jnp.where((sub < HALF) == low_half, kept, s_swap[...])
    map_outs.recv()
    for n in range(2 * nk):
        rows = slice((n % 2) * (TOK // 2), (n % 2 + 1) * (TOK // 2))
        map_grad[n // 2, rows, :] = m_groups[n].astype(F32)

    for swap in (swap_r, swap_g, relay_g, swap_c, swap_b, swap_w, swap_s):
        swap.wait_send()
    ring_w.sent()
    ring_i.sent()
    for family in (
        feats,
        feats_on,
        decays,
        adjoints.out,
        adjoints.back,
        scan.out,
        scan.back,
        columns_out,
        tcols,
        tcols_on,
        y_sibs,
        y_outs,
        map_parts,
        map_outs,
        pieces,
    ):
        family.sent()
    swap_o.wait_recv()
    swap_o.wait_send()


def local(tokens, w, cot, b, c, raw, rate_log, skip):
    nz = lax.axis_size("tok") // 2
    nk = lax.axis_size("ch") // 2
    piece, rowt, chips = CH // nz, TOK // nk, 2 * nk
    vmem = pl.BlockSpec(memory_space=pltpu.VMEM)
    smem = pl.BlockSpec(memory_space=pltpu.SMEM)
    hbm = pl.BlockSpec(memory_space=pl.ANY)
    v = pltpu.VMEM

    def body(*refs):
        kernel(nz, nk, *refs)

    results = pl.pallas_call(
        body,
        out_shape=(
            jax.ShapeDtypeStruct((TOK, CH), BF16),
            jax.ShapeDtypeStruct((TOK, 2 * CH), BF16),
            jax.ShapeDtypeStruct((2 * HALF, TOK), F32),
            jax.ShapeDtypeStruct((nk, TOK, STATE), F32),
        ),
        in_specs=[hbm] * 6 + [smem] * 2,
        out_specs=(vmem,) * 4,
        scratch_shapes=[
            v((2 * nk, 2, TOK, CH), BF16),
            v((nz, 2, TOK, CH), BF16),
            v((nz, 2, CH, TOK), BF16),
            v((2 * nk, 2, nz, rowt, TOK), BF16),
            v((2 * nk, rowt, TOK), BF16),
            v((TOK, CH), BF16),
            v((TOK, CH), BF16),
            v((TOK, CH), BF16),
            v((TOK, STATE), BF16),
            v((TOK, STATE), BF16),
            v((2 * HALF, TOK), F32),
            v((2, TOK, CH), BF16),
            v((2, TOK, STATE), BF16),
            v((2, TOK, STATE), BF16),
            v((2, 2 * HALF, TOK), F32),
            v((1, TOK), F32),
            v((nz, 1, TOK), F32),
            v((2, nz, piece, STATE), BF16),
            v((2, nz, piece, STATE), BF16),
            v((2, nz, piece, STATE), BF16),
            v((2, nz, piece, STATE), BF16),
            v((2, CH, TOK), F32),
            v((2, CH, TOK), BF16),
            v((2, CH, TOK), BF16),
            v((2 * HALF, TOK, TOK), F32),
            v((2, TOK, TOK), F32),
            v((2, CH, TOK), F32),
            v((2, CH, TOK), F32),
            v((CH, STATE), F32),
            v((CH, STATE), F32),
            v((6, 2 * HALF, TOK), F32),
            v((2 * TOK, CH), BF16),
            v((2 * TOK, CH), F32),
            v((CH, 2 * TOK), F32),
            v((2, nk, 2, TOK, CH), BF16),
            v((nk, 2, TOK, CH), BF16),
            v((nk, 2, TOK, CH), BF16),
            v((chips, TOK, CH), BF16),
            v((2, 2, TOK // 2, STATE), F32),
            v((4, TOK // 2, STATE), F32),
            v((2 * nk, TOK // 2, STATE), BF16),
            v((2, 2 * HALF, TOK), F32),
            v((2 * HALF, TOK), F32),
            v((2, TOK, CH), BF16),
            pltpu.SemaphoreType.DMA((11,)),
            pltpu.SemaphoreType.DMA((25,)),
            pltpu.SemaphoreType.DMA((23 + 16 * (nz // 2 + 1),)),
        ],
        compiler_params=pltpu.CompilerParams(
            collective_id=0, has_side_effects=True, vmem_limit_bytes=60 * 1024 * 1024
        ),
        name="mixer_backward",
    )(tokens, w, cot, b, c, raw, rate_log.reshape(1, 2 * HALF), skip.reshape(1, 2 * HALF))

    def hand_over(*refs):
        copies = [
            pltpu.make_async_copy(refs[n], refs[4 + n], refs[8].at[n]) for n in range(4)
        ]
        for copy in copies:
            copy.start()
        for copy in copies:
            copy.wait()

    return pl.pallas_call(
        hand_over,
        out_shape=tuple(jax.ShapeDtypeStruct(a.shape, a.dtype) for a in results),
        in_specs=[hbm] * 4,
        out_specs=(hbm,) * 4,
        scratch_shapes=[pltpu.SemaphoreType.DMA((4,))],
        compiler_params=pltpu.CompilerParams(vmem_limit_bytes=60 * 1024 * 1024),
        name="outputs",
    )(*results)


def solution(mesh):
    return jax.shard_map(
        local,
        mesh=mesh,
        in_specs=(
            P("tok", "ch"),
            P("tok", "ch"),
            P("tok", "ch"),
            P(None, "tok", None),
            P(None, "tok", None),
            P("ch", "tok"),
            P("ch"),
            P("ch"),
        ),
        out_specs=(P("tok", "ch"), P("tok", "ch"), P("ch", "tok"), P(None, "tok", None)),
        check_vma=False,
    )
```

```python
import jax
import jax.numpy as jnp
from jax import lax
from jax.experimental import pallas as pl
from jax.experimental.pallas import tpu as pltpu
from jax.sharding import PartitionSpec as P

MESH = pl.DeviceIdType.MESH
HIGHEST = lax.Precision.HIGHEST
F32 = jnp.float32
BF16 = jnp.bfloat16
TOK = 128
HEAD = 64
HALF = 4
CH = HALF * HEAD
STATE = 128

NN = (((1,), (0,)), ((), ()))
NT = (((1,), (1,)), ((), ()))


def dot(a, b, dims=NN):
    return lax.dot_general(a, b, dims, preferred_element_type=F32)


def dot2(a, b, dims=NN):
    high = a.astype(BF16)
    low = (a - high.astype(F32)).astype(BF16)
    return dot(high, b, dims) + dot(low, b, dims)


def dot_exact(a, b):
    return lax.dot_general(a, b, NN, precision=HIGHEST, preferred_element_type=F32)


def heads_to_rows(rows, p):
    return jnp.concatenate(
        [
            jnp.broadcast_to(rows[p * HALF + i : p * HALF + i + 1], (HEAD, rows.shape[1]))
            for i in range(HALF)
        ],
        axis=0,
    )


def kernel(
    nz,
    nk,
    tokens,
    w,
    cot,
    b_in,
    c_in,
    raw_in,
    rate_log,
    skip_in,
    token_grad,
    weight_grad,
    step_grad,
    map_grad,
    feat,
    wg,
    ig,
    tcol,
    tpre,
    w_other,
    cot_other,
    g_relay,
    b_other,
    c_other,
    raw_own,
    g,
    bs,
    cs,
    raw,
    dtile,
    dall,
    send_state,
    recv_state,
    back_state,
    state_in,
    gte,
    gtb,
    xtb,
    dec,
    inter,
    back_local,
    abt,
    a_last,
    s_first,
    vecs,
    igtm,
    proj,
    wtot,
    y_all,
    y_sib,
    y_out,
    y_in,
    m_own,
    m_in,
    m_groups,
    s_out,
    s_swap,
    wgrad,
    local_sem,
    send_sem,
    recv_sem,
):
    tok, c = lax.axis_index("tok"), lax.axis_index("ch")
    z, r = tok // 2, tok % 2
    k, core = c // 2, c % 2
    piece = CH // nz
    rowt = TOK // nk
    chips = 2 * nk
    hops = nz // 2
    partner = z * 2 + 1 - r
    sibling = c + 1 - 2 * core
    across = lax.rem(k + nk // 2, nk)
    low = k // (nk // 2)
    r_before = low * r + (1 - low) * (1 - r)
    r_after = low * (1 - r) + (1 - low) * r
    mine = pl.ds(pl.multiple_of(r * CH, CH), CH)
    other = pl.ds(pl.multiple_of((1 - r) * CH, CH), CH)
    me = r * nk + k

    def piece_of(kk, side):
        return (
            pl.ds(pl.multiple_of(kk * rowt, rowt), rowt),
            pl.ds(pl.multiple_of(side * TOK, TOK), TOK),
        )

    def ztok(zz, rr):
        return lax.rem(zz + nz, nz) * 2 + rr

    def xor(a, b, n):
        out, bit = 0, 1
        while bit < n:
            pa, pb = (a // bit) % 2, (b // bit) % 2
            out = out + bit * ((pa + pb) % 2)
            bit *= 2
        return out

    def chip(j):
        return (r + j // nk) % 2, xor(k, j % nk, nk)

    sends, recvs = [0], [0]

    def take(counter, n=1):
        counter[0] += n
        return counter[0] - n

    def remote(src, dst, s, q, tok_to, ch_to):
        return pltpu.make_async_remote_copy(
            src_ref=src,
            dst_ref=dst,
            send_sem=send_sem.at[s],
            recv_sem=recv_sem.at[q],
            device_id=(tok_to, ch_to),
            device_id_type=MESH,
        )

    def single(src, dst, tok_to, ch_to):
        return remote(src, dst, take(sends), take(recvs), tok_to, ch_to)

    def each(first, last, f):
        def body(j, carry):
            f(j)
            return carry

        lax.fori_loop(first, last, body, 0)

    class Family:
        def __init__(self, first, last, make, whole):
            self.first, self.last, self.whole = first, last, whole
            self.s, self.q = take(sends), take(recvs)
            self.make = lambda j: remote(*make(j)[:2], self.s, self.q, *make(j)[2:])
            self.all = lambda: remote(whole, whole, self.s, self.q, tok, sibling)

        def start(self):
            each(self.first, self.last, lambda j: self.make(j).start())

        def start_one(self, j):
            self.make(j).start()

        def recv(self):
            self.all().wait_recv()

        def sent(self):
            self.all().wait_send()

    class Ring:
        def __init__(self, buf, first):
            self.buf, self.first = buf, first
            self.rows = buf.shape[2] // 2
            self.s, self.q = take(sends), take(recvs, 8 * (hops + 1))

        def copy(self, way, s, n):
            block = lax.rem(z - way * (s - 1) + 2 * nz, nz)
            side = lax.rem(self.first + n // 2, 2)
            at = self.buf.at[block, side, pl.ds((n % 2) * self.rows, self.rows)]
            q = self.q + (s * 2 + (0 if way == 1 else 1)) * 4 + n
            return remote(at, at, self.s, q, ztok(z + way, r), c)

        def has(self, way, s, n):
            if s < hops:
                return True
            return s == hops and (n < 2) == (way == 1)

        def begin(self, n):
            for way in (1, -1):
                self.copy(way, 1, n).start()

        def tick(self, s, n):
            for way in (1, -1):
                if self.has(way, s, n):
                    self.copy(way, s, n).wait_recv()
                    if self.has(way, s + 1, n):
                        self.copy(way, s + 1, n).start()

        def ticks(self, group):
            for s, n in group:
                self.tick(s, n)

        def sent(self):
            whole = self.buf.at[pl.ds(0, nz - 1)]
            remote(whole, whole, self.s, self.q, tok, sibling).wait_send()

    loads = [
        pltpu.make_async_copy(src, dst, local_sem.at[n])
        for n, (src, dst) in enumerate(
            (
                (raw_in, raw_own),
                (cot.at[:, other], cot_other),
                (c_in.at[across], c_other),
                (w.at[:, mine], wg.at[z, r]),
                (w.at[:, other], w_other),
                (b_in.at[across], b_other),
                (tokens, feat.at[c, r]),
                (cot.at[:, mine], g.at[r]),
                (c_in.at[k], cs.at[r]),
                (b_in.at[k], bs.at[r]),
                (tokens.at[piece_of(k, core)], tpre.at[c]),
            )
        )
    ]
    for load in loads:
        load.start()

    barrier = pltpu.get_barrier_semaphore()

    def greet(tok_to, ch_to):
        pl.semaphore_signal(barrier, inc=1, device_id=(tok_to, ch_to), device_id_type=MESH)

    def greet_chip(j):
        rr, kk = chip(j)
        greet(z * 2 + rr, kk * 2 + core)

    each(1, nz, lambda j: greet(ztok(z + j, r), c))
    each(1, chips, greet_chip)
    each(1, nk, lambda j: greet(tok, xor(k, j, nk) * 2 + 1 - core))
    greet(tok, sibling)
    greet(partner, sibling)
    for load in loads:
        load.wait()
    pl.semaphore_wait(barrier, (nz - 1) + (chips - 1) + (nk - 1) + 2)

    ring_w = Ring(wg, r)
    swap_r = single(raw_own, raw.at[r], partner, c)
    swap_g = single(cot_other, g_relay, z * 2 + r_before, across * 2 + core)
    relay_g = single(g_relay, g.at[r_after], z * 2 + r_before, across * 2 + core)
    swap_c = single(c_other, cs.at[r], partner, across * 2 + core)
    swap_w = single(w_other, wg.at[z, r], partner, c)
    swap_b = single(b_other, bs.at[r], partner, across * 2 + core)
    swap_r.start()
    swap_g.start()
    swap_w.start()
    ring_w.begin(0)
    ring_w.begin(1)
    swap_c.start()
    swap_b.start()

    def piece_out(j):
        to = xor(c, j, 2 * nk)
        return feat.at[(c, r) + piece_of(to // 2, to % 2)], tpre.at[c], tok, to

    pieces = Family(1, 2 * nk, piece_out, tpre.at[pl.ds(0, 2 * nk - 1)])
    pieces.start()

    def feat_out(j):
        rr, kk = chip(j)
        at = feat.at[c, r]
        return at, at, z * 2 + rr, kk * 2 + core

    def feat_on(j):
        rr, kk = chip(j)
        at = feat.at[kk * 2 + core, rr]
        return at, at, tok, sibling

    feats = Family(1, chips, feat_out, feat.at[pl.ds(0, chips - 1), 0])
    feats_on = Family(0, chips, feat_on, feat.at[:, 0])
    raw[r] = raw_own[...]

    def own(t):
        if t <= hops:
            ring_w.ticks([(t, 0), (t, 1)])

    def far(t):
        if t <= hops:
            ring_w.ticks([(t, 2), (t, 3)])

    def grads(t):
        if t < hops or t == 8:
            ring_i.ticks([(min(t, hops), n) for n in range(4)])

    own(1)
    swap_r.wait_recv()

    low_half = r == 0
    rows = []
    for p in range(2):
        both = raw[p]
        rows.append(jnp.where(low_half, both[0:HALF], both[HALF : 2 * HALF]))
    raw8 = jnp.concatenate(rows, axis=0)
    steps = jnp.maximum(raw8, 0.0) + jnp.log1p(jnp.exp(-jnp.abs(raw8)))
    for i in range(HALF):
        rate = jnp.full((1, TOK), rate_log[0, r * HALF + i], F32)
        skip = jnp.full((1, TOK), skip_in[0, r * HALF + i], F32)
        for p in range(2):
            vecs[0, p * HALF + i : p * HALF + i + 1, :] = rate
            vecs[1, p * HALF + i : p * HALF + i + 1, :] = skip
    rates = -jnp.exp(vecs[0])
    skips = vecs[1]
    ids0 = lax.broadcasted_iota(jnp.int32, (TOK, TOK), 0)
    ids1 = lax.broadcasted_iota(jnp.int32, (TOK, TOK), 1)
    upto = (ids0 <= ids1).astype(F32)
    log_decay = dot_exact(steps * rates, upto)
    log_total = jnp.broadcast_to(log_decay[:, TOK - 1 : TOK], (2 * HALF, TOK))
    start_decay = jnp.exp(log_decay)
    end_decay = jnp.exp(log_total - log_decay)
    end_weight = end_decay * steps
    block_decay = jnp.exp(log_total)
    decay_rows = [heads_to_rows(block_decay, p) for p in range(2)]
    columns = jnp.concatenate([log_decay, jnp.zeros((TOK - 2 * HALF, TOK), F32)], axis=0).T
    lane = lax.broadcasted_iota(jnp.int32, (1, TOK), 1)
    decay_row = jnp.zeros((1, TOK), F32)
    for i in range(HALF):
        decay_row = jnp.where(
            lane == i, block_decay[i : i + 1] * block_decay[HALF + i : HALF + i + 1], decay_row
        )
    dtile[...] = decay_row
    dall[z] = decay_row

    def decay_out(j):
        return dtile, dall.at[z], ztok(z + j, r), c

    decays = Family(1, nz, decay_out, dall.at[pl.ds(0, nz - 1)])
    decays.start()
    swap_g.wait_recv()
    relay_g.start()
    own(2)
    relay_g.wait_recv()
    swap_c.wait_recv()
    adjoint = []
    for p in range(2):
        gt = g[p].astype(F32).T
        gtb[p] = gt.astype(BF16)
        gte[p] = gt * heads_to_rows(start_decay, p)
        adjoint.append(dot2(gte[p], cs[p]))
    a_last[...] = adjoint[1]

    class Exchange:
        def __init__(self, n, reverse):
            self.n, self.reverse = n, reverse

            def out(j):
                to = lax.rem(z + j, nz)
                return send_state.at[n, to], recv_state.at[n, z], ztok(to, r), c

            def back(j):
                to = lax.rem(z + j, nz)
                return back_state.at[n, to], state_in.at[n, z], ztok(to, r), c

            self.out = Family(1, nz, out, recv_state.at[n, pl.ds(0, nz - 1)])
            self.back = Family(1, nz, back, state_in.at[n, pl.ds(0, nz - 1)])

        def start(self, whole):
            n = self.n
            send_state[n] = whole.astype(BF16).reshape(nz, piece, STATE)
            self.out.start()
            recv_state[n, z] = send_state[n, z]

        def prefix(self):
            n = self.n
            head = (z * piece) // HEAD
            self.out.recv()
            carry = jnp.zeros((piece, STATE), F32)
            own = jnp.where(lane == head, dall[...].reshape(nz, TOK), 0.0)
            decay = jnp.broadcast_to(jnp.sum(own, axis=1, keepdims=True), (nz, STATE))
            for at in reversed(range(nz)) if self.reverse else range(nz):
                back_state[n, at] = carry.astype(BF16)
                carry = decay[at : at + 1] * carry + recv_state[n, at].astype(F32)
            self.back.start()
            state_in[n, z] = back_state[n, z]

        def result(self):
            self.back.recv()
            return state_in[self.n].astype(F32).reshape(CH, STATE)

    adjoints = Exchange(0, True)
    adjoints.start(adjoint[0] + decay_rows[0] * adjoint[1])
    swap_w.wait_recv()
    ring_w.begin(2)
    ring_w.begin(3)
    own(3)
    feats.start()
    feats_on.start_one(0)
    swap_b.wait_recv()

    lower = ids0 >= ids1

    def block_kernels(p, heads):
        if heads[0] == 0:
            inter[p] = dot(cs[p], bs[p], NT)
        for i in heads:
            q = p * HALF + i
            gap = columns[:, q : q + 1] - log_decay[q : q + 1, :]
            dec[q] = jnp.where(lower, jnp.exp(jnp.minimum(gap, 0.0)), 0.0)
            kern = (dec[q] * inter[p]).astype(BF16)
            back_local[p, i * HEAD : (i + 1) * HEAD, :] = dot(
                gtb[p, i * HEAD : (i + 1) * HEAD, :], kern
            )

    kept = {}

    def column_out(j):
        to = lax.rem(z + j, nz)
        return tpre.at[to], tcol.at[me, core, z], ztok(to, r), c

    def tcol_out(j):
        rr, kk = chip(j)
        at = tcol.at[me, core]
        return at, at, z * 2 + rr, kk * 2 + core

    def tcol_on(j):
        rr, kk = chip(j)
        at = tcol.at[rr * nk + kk, core]
        return at, at, tok, sibling

    columns_out = Family(1, nz, column_out, tcol.at[0, 0, pl.ds(0, nz - 1)])
    tcols = Family(1, chips, tcol_out, tcol.at[pl.ds(0, chips - 1), 0])
    tcols_on = Family(0, chips, tcol_on, tcol.at[:, 0])
    ring_i = Ring(ig, 0)
    scan = Exchange(1, False)

    def adjoint_prefix():
        decays.recv()
        adjoints.prefix()

    def columns_start():
        pieces.recv()
        columns_out.start()
        tcol[me, core, z] = tpre[z]

    def columns_spread():
        columns_out.recv()
        tcols.start()
        tcols_on.start_one(0)

    def features_on():
        feats.recv()
        each(1, chips, feats_on.start_one)

    def input_grads():
        late = adjoints.result()
        kept["adjoint"] = adjoint_at = [decay_rows[1] * late + a_last[...], late]
        for p in range(2):
            abt[p] = dot2(adjoint_at[p], bs[p], NT)
            back = back_local[p] + heads_to_rows(end_decay, p) * abt[p]
            grad = heads_to_rows(skips, p) * gtb[p].astype(F32) + heads_to_rows(steps, p) * back
            grad_low = grad.astype(BF16)
            ig[z, p] = grad_low
            ring_i.begin(2 * p)
            ring_i.begin(2 * p + 1)
            igtm[p * TOK : (p + 1) * TOK, :] = grad_low.astype(F32).T.astype(BF16)

    def project(first, last):
        last = min(last, hops + 1)
        total = proj[...] if first else jnp.zeros((2 * TOK, CH), F32)
        for d in range(first, last):
            for way in (1, -1) if 0 < d < hops else (1,):
                n = lax.rem(z + way * d + nz, nz)
                total = total + dot(feat[n].reshape(2 * TOK, CH), wg[n].reshape(CH, CH))
        proj[...] = total

    def scan_start():
        states = []
        for p in range(2):
            xt = proj[p * TOK : (p + 1) * TOK, :].astype(BF16).astype(F32).T
            xtb[p] = xt.astype(BF16)
            states.append(dot2(xt * heads_to_rows(end_weight, p), bs[p]))
        s_first[...] = states[0]
        scan.start(decay_rows[1] * states[0] + states[1])

    def term(kk, side):
        n = kk * 2 + side
        out = dot(igtm[...], wg[n].reshape(CH, CH), NT)
        y_all[side, kk] = out.astype(BF16).reshape(2, TOK, CH)

    def y_to_sibling(j):
        return y_all.at[1 - core, j], y_sib.at[j], tok, sibling

    def y_chip(j):
        rr, kk = chip(j)
        return y_out.at[kk, rr], y_in.at[j], z * 2 + rr, kk * 2 + core

    y_sibs = Family(0, nk, y_to_sibling, y_sib)
    y_outs = Family(1, chips, y_chip, y_in.at[pl.ds(1, chips - 1)])

    def first_terms():
        def one(j):
            term(j, 1 - core)
            y_sibs.start_one(j)

        each(0, nk, one)

    def own_terms():
        each(0, nk, lambda j: term(j, core))

    def y_sums():
        def one(j):
            y_out[j] = (y_all[core, j].astype(F32) + y_sib[j].astype(F32)).astype(BF16)

        y_sibs.recv()
        each(0, nk, one)
        y_in[0] = y_out[k, r]
        y_outs.start()

    def gather(first, last):
        last = min(last, hops + 1)
        total = wtot[...] if first else jnp.zeros((CH, 2 * TOK), F32)
        for d in range(first, last):
            for way in (1, -1) if 0 < d < hops else (1,):
                n = lax.rem(z + way * d + nz, nz)
                grad = jnp.concatenate([ig[n, 0], ig[n, 1]], axis=1)
                cols = [tcol[:, half, n].reshape(2 * TOK, TOK) for half in range(2)]
                total = total + dot(grad, jnp.concatenate(cols, axis=1))
        wtot[...] = total

    block_kernels(0, (0, 1, 2, 3))
    far(1)
    own(4)
    block_kernels(1, (0, 1, 2, 3))
    adjoint_prefix()
    far(2)
    own(5)
    columns_start()
    far(3)
    own(6)
    far(4)
    own(7)
    input_grads()
    far(5)
    own(8)
    features_on()
    columns_spread()
    far(6)
    grads(1)
    feats_on.recv()
    project(0,6)
    far(7)
    grads(2)
    project(6,7)
    far(8)
    project(7,9)
    scan_start()
    grads(3)
    first_terms()
    own_terms()
    grads(4)
    scan.prefix()
    y_sums()
    grads(5)
    adjoint_at = kept["adjoint"]

    rowsums = jnp.zeros((TOK, TOK), F32)
    colsums, ends, maps = [], [], []

    def pairs(p, heads, pair_sum, rowsums):
        for i in heads:
            q = p * HALF + i
            span = slice(i * HEAD, (i + 1) * HEAD)
            cross = dot(g[p, :, span], xtb[p, span, :])
            weights = dec[q] * cross
            pair_sum = pair_sum + weights * steps[q : q + 1, :]
            both = weights * inter[p]
            colsums.append(jnp.sum(both, axis=0, keepdims=True))
            row = jnp.sum(both * steps[q : q + 1, :], axis=1, keepdims=True)
            rowsums = jnp.where(ids1 == q, jnp.broadcast_to(row, (TOK, TOK)), rowsums)
            ends.append(
                jnp.sum(xtb[p, span, :].astype(F32) * abt[p, span, :], axis=0, keepdims=True)
            )
        return pair_sum, rowsums

    def pairs_of(p):
        pair_sum, kept["rows"] = pairs(
            p, (0, 1, 2, 3), jnp.zeros((TOK, TOK), F32), kept.get("rows", rowsums)
        )
        maps.append(dot2(pair_sum, bs[p]))

    pairs_of(0)
    pairs_of(1)
    grads(6)
    tcols.recv()
    each(1, chips, tcols_on.start_one)
    grads(7)
    rowsums = kept["rows"].T[0 : 2 * HALF]

    early = scan.result()
    state_at = [early, decay_rows[0] * early + s_first[...]]
    starts, corners = [], []
    for p in range(2):
        at_c = dot2(state_at[p], cs[p], NT)
        gs = gte[p]
        maps[p] = maps[p] + dot2(gs.T, state_at[p].astype(BF16))
        meets = adjoint_at[p] * state_at[p]
        for i in range(HALF):
            span = slice(i * HEAD, (i + 1) * HEAD)
            starts.append(jnp.sum(gs[span] * at_c[span], axis=0, keepdims=True))
            lanes = jnp.sum(meets[span], axis=0, keepdims=True)
            corners.append(
                jnp.broadcast_to(jnp.sum(lanes, axis=1, keepdims=True), (1, TOK))
            )
        m_own[p] = maps[p].reshape(2, TOK // 2, STATE)

    def map_to(j):
        rr, cc = (r + j // 2) % 2, (core + j % 2) % 2
        return m_own.at[rr, cc], m_in.at[j], z * 2 + rr, 2 * k + cc

    map_parts = Family(1, 4, map_to, m_in.at[pl.ds(1, 3)])
    map_parts.start()
    tcols_on.recv()
    gather(0, hops)
    grads(8)
    gather(hops, hops + 1)
    for half in range(2):
        wgrad[half] = wtot[:, half * TOK : (half + 1) * TOK].T.astype(BF16)
    swap_o = single(wgrad.at[1 - r], weight_grad.at[:, mine], partner, c)
    swap_o.start()
    weight_grad[:, mine] = wgrad[r]

    for n, parts in enumerate((colsums, ends, starts, corners)):
        for q in range(2 * HALF):
            vecs[2 + n, q : q + 1, :] = parts[q]
    colsum, end, start, corner = vecs[2], vecs[3], vecs[4], vecs[5]
    input_term = colsum + end_decay * end
    onward = (ids0 >= ids1).astype(F32)
    before = (ids0 < ids1).astype(F32)
    decay_term = (
        dot_exact(rowsums + start - steps * colsum, onward)
        + dot_exact(end_weight * end, before)
        + block_decay * corner
    )
    sigmoid = 1.0 / (1.0 + jnp.exp(-raw8))
    grads = sigmoid * (input_term + rates * decay_term)
    s_out[0, 0:HALF, :] = grads[0:HALF]
    s_out[0, HALF : 2 * HALF, :] = grads[0:HALF]
    s_out[1, 0:HALF, :] = grads[HALF : 2 * HALF]
    s_out[1, HALF : 2 * HALF, :] = grads[HALF : 2 * HALF]
    swap_s = single(s_out.at[1 - r], s_swap, partner, c)
    swap_s.start()

    map_parts.recv()
    m_groups[c] = (m_own[r, core] + m_in[1] + m_in[2] + m_in[3]).astype(BF16)

    def map_out(j):
        return m_groups.at[c], m_groups.at[c], tok, xor(c, j, 2 * nk)

    map_outs = Family(1, 2 * nk, map_out, m_groups.at[pl.ds(0, 2 * nk - 1)])
    map_outs.start()

    y_outs.recv()
    total = y_in[0].astype(F32)
    for j in range(1, chips):
        total = total + y_in[j].astype(F32)
    token_grad[...] = total.astype(BF16)
    swap_s.wait_recv()
    mixed = jnp.where(low_half, s_out[0], s_out[1])
    sub = lax.broadcasted_iota(jnp.int32, (2 * HALF, TOK), 0)
    step_grad[...] = jnp.where((sub < HALF) == low_half, mixed, s_swap[...])
    map_outs.recv()
    for n in range(2 * nk):
        rows = slice((n % 2) * (TOK // 2), (n % 2 + 1) * (TOK // 2))
        map_grad[n // 2, rows, :] = m_groups[n].astype(F32)

    for swap in (swap_r, swap_g, relay_g, swap_c, swap_b, swap_w, swap_s):
        swap.wait_send()
    ring_w.sent()
    ring_i.sent()
    for family in (
        feats,
        feats_on,
        decays,
        adjoints.out,
        adjoints.back,
        scan.out,
        scan.back,
        columns_out,
        tcols,
        tcols_on,
        y_sibs,
        y_outs,
        map_parts,
        map_outs,
        pieces,
    ):
        family.sent()
    swap_o.wait_recv()
    swap_o.wait_send()


def local(tokens, w, cot, b, c, raw, rate_log, skip):
    nz = lax.axis_size("tok") // 2
    nk = lax.axis_size("ch") // 2
    piece, rowt, chips = CH // nz, TOK // nk, 2 * nk
    vmem = pl.BlockSpec(memory_space=pltpu.VMEM)
    smem = pl.BlockSpec(memory_space=pltpu.SMEM)
    hbm = pl.BlockSpec(memory_space=pl.ANY)
    v = pltpu.VMEM

    def body(*refs):
        kernel(nz, nk, *refs)

    results = pl.pallas_call(
        body,
        out_shape=(
            jax.ShapeDtypeStruct((TOK, CH), BF16),
            jax.ShapeDtypeStruct((TOK, 2 * CH), BF16),
            jax.ShapeDtypeStruct((2 * HALF, TOK), F32),
            jax.ShapeDtypeStruct((nk, TOK, STATE), F32),
        ),
        in_specs=[hbm] * 6 + [smem] * 2,
        out_specs=(vmem,) * 4,
        scratch_shapes=[
            v((2 * nk, 2, TOK, CH), BF16),
            v((nz, 2, TOK, CH), BF16),
            v((nz, 2, CH, TOK), BF16),
            v((2 * nk, 2, nz, rowt, TOK), BF16),
            v((2 * nk, rowt, TOK), BF16),
            v((TOK, CH), BF16),
            v((TOK, CH), BF16),
            v((TOK, CH), BF16),
            v((TOK, STATE), BF16),
            v((TOK, STATE), BF16),
            v((2 * HALF, TOK), F32),
            v((2, TOK, CH), BF16),
            v((2, TOK, STATE), BF16),
            v((2, TOK, STATE), BF16),
            v((2, 2 * HALF, TOK), F32),
            v((1, TOK), F32),
            v((nz, 1, TOK), F32),
            v((2, nz, piece, STATE), BF16),
            v((2, nz, piece, STATE), BF16),
            v((2, nz, piece, STATE), BF16),
            v((2, nz, piece, STATE), BF16),
            v((2, CH, TOK), F32),
            v((2, CH, TOK), BF16),
            v((2, CH, TOK), BF16),
            v((2 * HALF, TOK, TOK), F32),
            v((2, TOK, TOK), F32),
            v((2, CH, TOK), F32),
            v((2, CH, TOK), F32),
            v((CH, STATE), F32),
            v((CH, STATE), F32),
            v((6, 2 * HALF, TOK), F32),
            v((2 * TOK, CH), BF16),
            v((2 * TOK, CH), F32),
            v((CH, 2 * TOK), F32),
            v((2, nk, 2, TOK, CH), BF16),
            v((nk, 2, TOK, CH), BF16),
            v((nk, 2, TOK, CH), BF16),
            v((chips, TOK, CH), BF16),
            v((2, 2, TOK // 2, STATE), F32),
            v((4, TOK // 2, STATE), F32),
            v((2 * nk, TOK // 2, STATE), BF16),
            v((2, 2 * HALF, TOK), F32),
            v((2 * HALF, TOK), F32),
            v((2, TOK, CH), BF16),
            pltpu.SemaphoreType.DMA((11,)),
            pltpu.SemaphoreType.DMA((25,)),
            pltpu.SemaphoreType.DMA((23 + 16 * (nz // 2 + 1),)),
        ],
        compiler_params=pltpu.CompilerParams(
            collective_id=0, has_side_effects=True, vmem_limit_bytes=60 * 1024 * 1024
        ),
        name="mixer_backward",
    )(tokens, w, cot, b, c, raw, rate_log.reshape(1, 2 * HALF), skip.reshape(1, 2 * HALF))

    def hand_over(*refs):
        for first in (0, 8):
            copies = [
                pltpu.make_async_copy(refs[(first + n) % 12], refs[8 - first // 2 + n], refs[12].at[n])
                for n in range(4)
            ]
            for copy in copies:
                copy.start()
            for copy in copies:
                copy.wait()

    return pl.pallas_call(
        hand_over,
        out_shape=tuple(jax.ShapeDtypeStruct(a.shape, a.dtype) for a in results),
        in_specs=[hbm] * 4,
        out_specs=(hbm,) * 4,
        scratch_shapes=[v(a.shape, a.dtype) for a in results] + [pltpu.SemaphoreType.DMA((4,))],
        compiler_params=pltpu.CompilerParams(vmem_limit_bytes=60 * 1024 * 1024),
        name="outputs",
    )(*results)


def solution(mesh):
    return jax.shard_map(
        local,
        mesh=mesh,
        in_specs=(
            P("tok", "ch"),
            P("tok", "ch"),
            P("tok", "ch"),
            P(None, "tok", None),
            P(None, "tok", None),
            P("ch", "tok"),
            P("ch"),
            P("ch"),
        ),
        out_specs=(P("tok", "ch"), P("tok", "ch"), P("ch", "tok"), P(None, "tok", None)),
        check_vma=False,
    )
```

```python
import jax
import jax.numpy as jnp
from jax import lax
from jax.experimental import pallas as pl
from jax.experimental.pallas import tpu as pltpu
from jax.sharding import PartitionSpec as P

MESH = pl.DeviceIdType.MESH
HIGHEST = lax.Precision.HIGHEST
F32 = jnp.float32
BF16 = jnp.bfloat16
TOK = 128
HEAD = 64
HALF = 4
CH = HALF * HEAD
STATE = 128

NN = (((1,), (0,)), ((), ()))
NT = (((1,), (1,)), ((), ()))


def dot(a, b, dims=NN):
    return lax.dot_general(a, b, dims, preferred_element_type=F32)


def dot2(a, b, dims=NN):
    high = a.astype(BF16)
    low = (a - high.astype(F32)).astype(BF16)
    return dot(high, b, dims) + dot(low, b, dims)


def dot_exact(a, b):
    return lax.dot_general(a, b, NN, precision=HIGHEST, preferred_element_type=F32)


def heads_to_rows(rows, p):
    return jnp.concatenate(
        [
            jnp.broadcast_to(rows[p * HALF + i : p * HALF + i + 1], (HEAD, rows.shape[1]))
            for i in range(HALF)
        ],
        axis=0,
    )


def kernel(
    nz,
    nk,
    tokens,
    w,
    cot,
    b_in,
    c_in,
    raw_in,
    rate_log,
    skip_in,
    token_grad,
    weight_grad,
    step_grad,
    map_grad,
    feat,
    wg,
    ig,
    tcol,
    tpre,
    w_other,
    cot_other,
    g_relay,
    b_other,
    c_other,
    raw_own,
    g,
    bs,
    cs,
    raw,
    dtile,
    dall,
    send_state,
    recv_state,
    back_state,
    state_in,
    gte,
    gtb,
    gt_high,
    gt_low,
    xtb,
    dec,
    inter,
    back_local,
    abt,
    a_last,
    s_first,
    vecs,
    igtm,
    proj,
    wtot,
    y_all,
    y_sib,
    y_out,
    y_in,
    m_own,
    m_in,
    m_groups,
    s_out,
    s_swap,
    wgrad,
    local_sem,
    send_sem,
    recv_sem,
):
    tok, c = lax.axis_index("tok"), lax.axis_index("ch")
    z, r = tok // 2, tok % 2
    k, core = c // 2, c % 2
    piece = CH // nz
    rowt = TOK // nk
    chips = 2 * nk
    hops = nz // 2
    partner = z * 2 + 1 - r
    sibling = c + 1 - 2 * core
    across = lax.rem(k + nk // 2, nk)
    low = k // (nk // 2)
    r_before = low * r + (1 - low) * (1 - r)
    r_after = low * (1 - r) + (1 - low) * r
    mine = pl.ds(pl.multiple_of(r * CH, CH), CH)
    other = pl.ds(pl.multiple_of((1 - r) * CH, CH), CH)
    me = r * nk + k

    def piece_of(kk, side):
        return (
            pl.ds(pl.multiple_of(kk * rowt, rowt), rowt),
            pl.ds(pl.multiple_of(side * TOK, TOK), TOK),
        )

    def ztok(zz, rr):
        return lax.rem(zz + nz, nz) * 2 + rr

    def xor(a, b, n):
        out, bit = 0, 1
        while bit < n:
            pa, pb = (a // bit) % 2, (b // bit) % 2
            out = out + bit * ((pa + pb) % 2)
            bit *= 2
        return out

    def chip(j):
        return (r + j // nk) % 2, xor(k, j % nk, nk)

    def far_first(j):
        return hops + (1 - 2 * ((j - 1) % 2)) * (j // 2)

    sends, recvs = [0], [0]

    def take(counter, n=1):
        counter[0] += n
        return counter[0] - n

    def remote(src, dst, s, q, tok_to, ch_to):
        return pltpu.make_async_remote_copy(
            src_ref=src,
            dst_ref=dst,
            send_sem=send_sem.at[s],
            recv_sem=recv_sem.at[q],
            device_id=(tok_to, ch_to),
            device_id_type=MESH,
        )

    def single(src, dst, tok_to, ch_to):
        return remote(src, dst, take(sends), take(recvs), tok_to, ch_to)

    def each(first, last, f):
        def body(j, carry):
            f(j)
            return carry

        lax.fori_loop(first, last, body, 0)

    class Family:
        def __init__(self, first, last, make, whole):
            self.first, self.last, self.whole = first, last, whole
            self.s, self.q = take(sends), take(recvs)
            self.make = lambda j: remote(*make(j)[:2], self.s, self.q, *make(j)[2:])
            self.all = lambda: remote(whole, whole, self.s, self.q, tok, sibling)

        def start(self):
            each(self.first, self.last, lambda j: self.make(j).start())

        def start_one(self, j):
            self.make(j).start()

        def recv(self):
            self.all().wait_recv()

        def sent(self):
            self.all().wait_send()

    class Ring:
        def __init__(self, buf, first):
            self.buf, self.first = buf, first
            self.rows = buf.shape[2] // 2
            self.s, self.q = take(sends), take(recvs, 8 * (hops + 1))

        def copy(self, way, s, n):
            block = lax.rem(z - way * (s - 1) + 2 * nz, nz)
            side = lax.rem(self.first + n // 2, 2)
            at = self.buf.at[block, side, pl.ds((n % 2) * self.rows, self.rows)]
            q = self.q + (s * 2 + (0 if way == 1 else 1)) * 4 + n
            return remote(at, at, self.s, q, ztok(z + way, r), c)

        def has(self, way, s, n):
            if s < hops:
                return True
            return s == hops and (n < 2) == (way == 1)

        def begin(self, n):
            for way in (1, -1):
                self.copy(way, 1, n).start()

        def tick(self, s, n):
            for way in (1, -1):
                if self.has(way, s, n):
                    self.copy(way, s, n).wait_recv()
                    if self.has(way, s + 1, n):
                        self.copy(way, s + 1, n).start()

        def ticks(self, group):
            for s, n in group:
                self.tick(s, n)

        def sent(self):
            whole = self.buf.at[pl.ds(0, nz - 1)]
            remote(whole, whole, self.s, self.q, tok, sibling).wait_send()

    loads = [
        pltpu.make_async_copy(src, dst, local_sem.at[n])
        for n, (src, dst) in enumerate(
            (
                (raw_in, raw_own),
                (cot.at[:, other], cot_other),
                (c_in.at[across], c_other),
                (w.at[:, mine], wg.at[z, r]),
                (w.at[:, other], w_other),
                (b_in.at[across], b_other),
                (tokens, feat.at[c, r]),
                (cot.at[:, mine], g.at[r]),
                (c_in.at[k], cs.at[r]),
                (b_in.at[k], bs.at[r]),
                (tokens.at[piece_of(k, core)], tpre.at[c]),
            )
        )
    ]
    for load in loads:
        load.start()

    barrier = pltpu.get_barrier_semaphore()

    def greet(tok_to, ch_to):
        pl.semaphore_signal(barrier, inc=1, device_id=(tok_to, ch_to), device_id_type=MESH)

    def greet_chip(j):
        rr, kk = chip(j)
        greet(z * 2 + rr, kk * 2 + core)

    each(1, nz, lambda j: greet(ztok(z + j, r), c))
    each(1, chips, greet_chip)
    each(1, nk, lambda j: greet(tok, xor(k, j, nk) * 2 + 1 - core))
    greet(tok, sibling)
    greet(partner, sibling)
    for load in loads:
        load.wait()
    pl.semaphore_wait(barrier, (nz - 1) + (chips - 1) + (nk - 1) + 2)

    ring_w = Ring(wg, r)
    swap_r = single(raw_own, raw.at[r], partner, c)
    swap_g = single(cot_other, g_relay, z * 2 + r_before, across * 2 + core)
    relay_g = single(g_relay, g.at[r_after], z * 2 + r_before, across * 2 + core)
    swap_c = single(c_other, cs.at[r], partner, across * 2 + core)
    swap_w = single(w_other, wg.at[z, r], partner, c)
    swap_b = single(b_other, bs.at[r], partner, across * 2 + core)
    swap_r.start()
    swap_g.start()
    swap_w.start()
    ring_w.begin(0)
    ring_w.begin(1)
    swap_c.start()
    swap_b.start()

    def piece_out(j):
        to = xor(c, j, 2 * nk)
        return feat.at[(c, r) + piece_of(to // 2, to % 2)], tpre.at[c], tok, to

    pieces = Family(1, 2 * nk, piece_out, tpre.at[pl.ds(0, 2 * nk - 1)])
    pieces.start()

    def feat_out(j):
        rr, kk = chip(j)
        at = feat.at[c, r]
        return at, at, z * 2 + rr, kk * 2 + core

    def feat_on(j):
        rr, kk = chip(j)
        at = feat.at[kk * 2 + core, rr]
        return at, at, tok, sibling

    feats = Family(1, chips, feat_out, feat.at[pl.ds(0, chips - 1), 0])
    feats_on = Family(0, chips, feat_on, feat.at[:, 0])
    raw[r] = raw_own[...]

    def own(t):
        if t <= hops:
            ring_w.ticks([(t, 0), (t, 1)])

    def far(t):
        if t <= hops:
            ring_w.ticks([(t, 2), (t, 3)])

    def grads(t):
        if t < hops or t == 8:
            ring_i.ticks([(min(t, hops), n) for n in range(4)])

    own(1)
    swap_r.wait_recv()

    low_half = r == 0
    rows = []
    for p in range(2):
        both = raw[p]
        rows.append(jnp.where(low_half, both[0:HALF], both[HALF : 2 * HALF]))
    raw8 = jnp.concatenate(rows, axis=0)
    steps = jnp.maximum(raw8, 0.0) + jnp.log1p(jnp.exp(-jnp.abs(raw8)))
    for i in range(HALF):
        rate = jnp.full((1, TOK), rate_log[0, r * HALF + i], F32)
        skip = jnp.full((1, TOK), skip_in[0, r * HALF + i], F32)
        for p in range(2):
            vecs[0, p * HALF + i : p * HALF + i + 1, :] = rate
            vecs[1, p * HALF + i : p * HALF + i + 1, :] = skip
    rates = -jnp.exp(vecs[0])
    skips = vecs[1]
    ids0 = lax.broadcasted_iota(jnp.int32, (TOK, TOK), 0)
    ids1 = lax.broadcasted_iota(jnp.int32, (TOK, TOK), 1)
    upto = (ids0 <= ids1).astype(F32)
    log_decay = dot_exact(steps * rates, upto)
    log_total = jnp.broadcast_to(log_decay[:, TOK - 1 : TOK], (2 * HALF, TOK))
    start_decay = jnp.exp(log_decay)
    end_decay = jnp.exp(log_total - log_decay)
    end_weight = end_decay * steps
    block_decay = jnp.exp(log_total)
    decay_rows = [heads_to_rows(block_decay, p) for p in range(2)]
    columns = jnp.concatenate([log_decay, jnp.zeros((TOK - 2 * HALF, TOK), F32)], axis=0).T
    lane = lax.broadcasted_iota(jnp.int32, (1, TOK), 1)
    decay_row = jnp.zeros((1, TOK), F32)
    for i in range(HALF):
        decay_row = jnp.where(
            lane == i, block_decay[i : i + 1] * block_decay[HALF + i : HALF + i + 1], decay_row
        )
    dtile[...] = decay_row
    dall[z] = decay_row

    def decay_out(j):
        return dtile, dall.at[z], ztok(z + far_first(j), r), c

    decays = Family(1, nz, decay_out, dall.at[pl.ds(0, nz - 1)])
    decays.start()
    swap_g.wait_recv()
    relay_g.start()
    own(2)
    relay_g.wait_recv()
    swap_c.wait_recv()
    adjoint = []
    for p in range(2):
        gt = g[p].astype(F32).T
        gtb[p] = gt.astype(BF16)
        gte[p] = gt * heads_to_rows(start_decay, p)
        adjoint.append(dot2(gte[p], cs[p]))
    a_last[...] = adjoint[1]

    class Exchange:
        def __init__(self, n, reverse):
            self.n, self.reverse = n, reverse

            def out(j):
                to = lax.rem(z + far_first(j), nz)
                return send_state.at[n, to], recv_state.at[n, z], ztok(to, r), c

            def back(j):
                to = lax.rem(z + far_first(j), nz)
                return back_state.at[n, to], state_in.at[n, z], ztok(to, r), c

            self.out = Family(1, nz, out, recv_state.at[n, pl.ds(0, nz - 1)])
            self.back = Family(1, nz, back, state_in.at[n, pl.ds(0, nz - 1)])

        def start(self, whole):
            n = self.n
            send_state[n] = whole.astype(BF16).reshape(nz, piece, STATE)
            self.out.start()
            recv_state[n, z] = send_state[n, z]

        def prefix(self):
            n = self.n
            head = (z * piece) // HEAD
            self.out.recv()
            carry = jnp.zeros((piece, STATE), F32)
            own = jnp.where(lane == head, dall[...].reshape(nz, TOK), 0.0)
            decay = jnp.broadcast_to(jnp.sum(own, axis=1, keepdims=True), (nz, STATE))
            for at in reversed(range(nz)) if self.reverse else range(nz):
                back_state[n, at] = carry.astype(BF16)
                carry = decay[at : at + 1] * carry + recv_state[n, at].astype(F32)
            self.back.start()
            state_in[n, z] = back_state[n, z]

        def result(self):
            self.back.recv()
            return state_in[self.n].astype(F32).reshape(CH, STATE)

    adjoints = Exchange(0, True)
    adjoints.start(adjoint[0] + decay_rows[0] * adjoint[1])
    swap_w.wait_recv()
    ring_w.begin(2)
    ring_w.begin(3)
    own(3)
    feats.start()
    feats_on.start_one(0)
    swap_b.wait_recv()

    lower = ids0 >= ids1

    def block_kernels(p, heads):
        if heads[0] == 0:
            inter[p] = dot(cs[p], bs[p], NT)
        for i in heads:
            q = p * HALF + i
            gap = columns[:, q : q + 1] - log_decay[q : q + 1, :]
            dec[q] = jnp.where(lower, jnp.exp(jnp.minimum(gap, 0.0)), 0.0)
            kern = (dec[q] * inter[p]).astype(BF16)
            back_local[p, i * HEAD : (i + 1) * HEAD, :] = dot(
                gtb[p, i * HEAD : (i + 1) * HEAD, :], kern
            )

    kept = {}

    def column_out(j):
        to = lax.rem(z + far_first(j), nz)
        return tpre.at[to], tcol.at[me, core, z], ztok(to, r), c

    def tcol_out(j):
        rr, kk = chip(j)
        at = tcol.at[me, core]
        return at, at, z * 2 + rr, kk * 2 + core

    def tcol_on(j):
        rr, kk = chip(j)
        at = tcol.at[rr * nk + kk, core]
        return at, at, tok, sibling

    columns_out = Family(1, nz, column_out, tcol.at[0, 0, pl.ds(0, nz - 1)])
    tcols = Family(1, chips, tcol_out, tcol.at[pl.ds(0, chips - 1), 0])
    tcols_on = Family(0, chips, tcol_on, tcol.at[:, 0])
    ring_i = Ring(ig, 0)
    scan = Exchange(1, False)

    def adjoint_prefix():
        decays.recv()
        adjoints.prefix()

    def columns_start():
        pieces.recv()
        columns_out.start()
        tcol[me, core, z] = tpre[z]

    def columns_spread():
        columns_out.recv()
        tcols.start()
        tcols_on.start_one(0)

    def features_on():
        feats.recv()
        each(1, chips, feats_on.start_one)

    def input_grads():
        late = adjoints.result()
        kept["adjoint"] = adjoint_at = [decay_rows[1] * late + a_last[...], late]
        for p in range(2):
            abt[p] = dot2(adjoint_at[p], bs[p], NT)
            back = back_local[p] + heads_to_rows(end_decay, p) * abt[p]
            grad = heads_to_rows(skips, p) * gtb[p].astype(F32) + heads_to_rows(steps, p) * back
            grad_low = grad.astype(BF16)
            ig[z, p] = grad_low
            ring_i.begin(2 * p)
            ring_i.begin(2 * p + 1)
            igtm[p * TOK : (p + 1) * TOK, :] = grad_low.astype(F32).T.astype(BF16)

    def project(first, last):
        last = min(last, hops + 1)
        total = proj[...] if first else jnp.zeros((2 * TOK, CH), F32)
        for d in range(first, last):
            for way in (1, -1) if 0 < d < hops else (1,):
                n = lax.rem(z + way * d + nz, nz)
                total = total + dot(feat[n].reshape(2 * TOK, CH), wg[n].reshape(CH, CH))
        proj[...] = total

    def scan_start():
        states = []
        for p in range(2):
            xt = proj[p * TOK : (p + 1) * TOK, :].astype(BF16).astype(F32).T
            xtb[p] = xt.astype(BF16)
            states.append(dot2(xt * heads_to_rows(end_weight, p), bs[p]))
        s_first[...] = states[0]
        scan.start(decay_rows[1] * states[0] + states[1])

    def term(kk, side):
        n = kk * 2 + side
        out = dot(igtm[...], wg[n].reshape(CH, CH), NT)
        y_all[side, kk] = out.astype(BF16).reshape(2, TOK, CH)

    def y_to_sibling(j):
        return y_all.at[1 - core, j], y_sib.at[j], tok, sibling

    def y_chip(j):
        rr, kk = chip(j)
        return y_out.at[kk, rr], y_in.at[j], z * 2 + rr, kk * 2 + core

    y_sibs = Family(0, nk, y_to_sibling, y_sib)
    y_outs = Family(1, chips, y_chip, y_in.at[pl.ds(1, chips - 1)])

    def first_terms():
        def one(j):
            term(j, 1 - core)
            y_sibs.start_one(j)

        each(0, nk, one)

    def own_terms():
        each(0, nk, lambda j: term(j, core))

    def y_sums():
        def one(j):
            y_out[j] = (y_all[core, j].astype(F32) + y_sib[j].astype(F32)).astype(BF16)

        y_sibs.recv()
        each(0, nk, one)
        y_in[0] = y_out[k, r]
        y_outs.start()

    def gather(first, last):
        last = min(last, hops + 1)
        total = wtot[...] if first else jnp.zeros((CH, 2 * TOK), F32)
        for d in range(first, last):
            for way in (1, -1) if 0 < d < hops else (1,):
                n = lax.rem(z + way * d + nz, nz)
                grad = jnp.concatenate([ig[n, 0], ig[n, 1]], axis=1)
                cols = [tcol[:, half, n].reshape(2 * TOK, TOK) for half in range(2)]
                total = total + dot(grad, jnp.concatenate(cols, axis=1))
        wtot[...] = total

    block_kernels(0, (0, 1, 2, 3))
    far(1)
    own(4)
    block_kernels(1, (0, 1, 2, 3))
    adjoint_prefix()
    far(2)
    own(5)
    columns_start()
    far(3)
    own(6)
    far(4)
    own(7)
    input_grads()
    far(5)
    own(8)
    features_on()
    columns_spread()
    far(6)
    grads(1)
    feats_on.recv()
    project(0,6)
    far(7)
    grads(2)
    project(6,7)
    far(8)
    project(7,9)
    scan_start()
    grads(3)
    first_terms()
    own_terms()
    grads(4)
    scan.prefix()
    y_sums()
    grads(5)
    adjoint_at = kept["adjoint"]

    rowsums = jnp.zeros((TOK, TOK), F32)
    colsums, ends, maps = [], [], []

    def pairs(p, heads, pair_sum, rowsums):
        for i in heads:
            q = p * HALF + i
            span = slice(i * HEAD, (i + 1) * HEAD)
            cross = dot(g[p, :, span], xtb[p, span, :])
            weights = dec[q] * cross
            pair_sum = pair_sum + weights * steps[q : q + 1, :]
            both = weights * inter[p]
            colsums.append(jnp.sum(both, axis=0, keepdims=True))
            row = jnp.sum(both * steps[q : q + 1, :], axis=1, keepdims=True)
            rowsums = jnp.where(ids1 == q, jnp.broadcast_to(row, (TOK, TOK)), rowsums)
            ends.append(
                jnp.sum(xtb[p, span, :].astype(F32) * abt[p, span, :], axis=0, keepdims=True)
            )
        return pair_sum, rowsums

    def pairs_of(p):
        pair_sum, kept["rows"] = pairs(
            p, (0, 1, 2, 3), jnp.zeros((TOK, TOK), F32), kept.get("rows", rowsums)
        )
        maps.append(dot2(pair_sum, bs[p]))
        turned = gte[p].T
        gt_high[p] = turned.astype(BF16)
        gt_low[p] = (turned - gt_high[p].astype(F32)).astype(BF16)

    pairs_of(0)
    pairs_of(1)
    grads(6)
    tcols.recv()
    each(1, chips, tcols_on.start_one)
    grads(7)
    rowsums = kept["rows"].T[0 : 2 * HALF]

    early = scan.result()
    state_at = [early, decay_rows[0] * early + s_first[...]]
    for p in range(2):
        low_state = state_at[p].astype(BF16)
        maps[p] = maps[p] + (dot(gt_high[p], low_state) + dot(gt_low[p], low_state))
        m_own[p] = maps[p].reshape(2, TOK // 2, STATE)

    def map_to(j):
        rr, cc = (r + j // 2) % 2, (core + j % 2) % 2
        return m_own.at[rr, cc], m_in.at[j], z * 2 + rr, 2 * k + cc

    map_parts = Family(1, 4, map_to, m_in.at[pl.ds(1, 3)])
    map_parts.start()

    starts, corners = [], []
    for p in range(2):
        at_c = dot2(state_at[p], cs[p], NT)
        gs = gte[p]
        meets = adjoint_at[p] * state_at[p]
        for i in range(HALF):
            span = slice(i * HEAD, (i + 1) * HEAD)
            starts.append(jnp.sum(gs[span] * at_c[span], axis=0, keepdims=True))
            lanes = jnp.sum(meets[span], axis=0, keepdims=True)
            corners.append(
                jnp.broadcast_to(jnp.sum(lanes, axis=1, keepdims=True), (1, TOK))
            )

    for n, parts in enumerate((colsums, ends, starts, corners)):
        for q in range(2 * HALF):
            vecs[2 + n, q : q + 1, :] = parts[q]
    colsum, end, start, corner = vecs[2], vecs[3], vecs[4], vecs[5]
    input_term = colsum + end_decay * end
    onward = (ids0 >= ids1).astype(F32)
    before = (ids0 < ids1).astype(F32)
    decay_term = (
        dot_exact(rowsums + start - steps * colsum, onward)
        + dot_exact(end_weight * end, before)
        + block_decay * corner
    )
    sigmoid = 1.0 / (1.0 + jnp.exp(-raw8))
    step_terms = sigmoid * (input_term + rates * decay_term)
    s_out[0, 0:HALF, :] = step_terms[0:HALF]
    s_out[0, HALF : 2 * HALF, :] = step_terms[0:HALF]
    s_out[1, 0:HALF, :] = step_terms[HALF : 2 * HALF]
    s_out[1, HALF : 2 * HALF, :] = step_terms[HALF : 2 * HALF]
    swap_s = single(s_out.at[1 - r], s_swap, partner, c)
    swap_s.start()

    tcols_on.recv()
    gather(0, hops)
    map_parts.recv()
    m_groups[c] = (m_own[r, core] + m_in[1] + m_in[2] + m_in[3]).astype(BF16)

    def map_out(j):
        return m_groups.at[c], m_groups.at[c], tok, xor(c, j, 2 * nk)

    map_outs = Family(1, 2 * nk, map_out, m_groups.at[pl.ds(0, 2 * nk - 1)])
    map_outs.start()

    grads(8)
    gather(hops, hops + 1)
    for half in range(2):
        wgrad[half] = wtot[:, half * TOK : (half + 1) * TOK].T.astype(BF16)
    swap_o = single(wgrad.at[1 - r], weight_grad.at[:, mine], partner, c)
    swap_o.start()
    weight_grad[:, mine] = wgrad[r]

    y_outs.recv()
    total = y_in[0].astype(F32)
    for j in range(1, chips):
        total = total + y_in[j].astype(F32)
    token_grad[...] = total.astype(BF16)
    swap_s.wait_recv()
    mixed = jnp.where(low_half, s_out[0], s_out[1])
    sub = lax.broadcasted_iota(jnp.int32, (2 * HALF, TOK), 0)
    step_grad[...] = jnp.where((sub < HALF) == low_half, mixed, s_swap[...])
    map_outs.recv()
    for n in range(2 * nk):
        rows = slice((n % 2) * (TOK // 2), (n % 2 + 1) * (TOK // 2))
        map_grad[n // 2, rows, :] = m_groups[n].astype(F32)

    for swap in (swap_r, swap_g, relay_g, swap_c, swap_b, swap_w, swap_s):
        swap.wait_send()
    ring_w.sent()
    ring_i.sent()
    for family in (
        feats,
        feats_on,
        decays,
        adjoints.out,
        adjoints.back,
        scan.out,
        scan.back,
        columns_out,
        tcols,
        tcols_on,
        y_sibs,
        y_outs,
        map_parts,
        map_outs,
        pieces,
    ):
        family.sent()
    swap_o.wait_recv()
    swap_o.wait_send()


def local(tokens, w, cot, b, c, raw, rate_log, skip):
    nz = lax.axis_size("tok") // 2
    nk = lax.axis_size("ch") // 2
    piece, rowt, chips = CH // nz, TOK // nk, 2 * nk
    vmem = pl.BlockSpec(memory_space=pltpu.VMEM)
    smem = pl.BlockSpec(memory_space=pltpu.SMEM)
    hbm = pl.BlockSpec(memory_space=pl.ANY)
    v = pltpu.VMEM

    def body(*refs):
        kernel(nz, nk, *refs)

    results = pl.pallas_call(
        body,
        out_shape=(
            jax.ShapeDtypeStruct((TOK, CH), BF16),
            jax.ShapeDtypeStruct((TOK, 2 * CH), BF16),
            jax.ShapeDtypeStruct((2 * HALF, TOK), F32),
            jax.ShapeDtypeStruct((nk, TOK, STATE), F32),
        ),
        in_specs=[hbm] * 6 + [smem] * 2,
        out_specs=(vmem,) * 4,
        scratch_shapes=[
            v((2 * nk, 2, TOK, CH), BF16),
            v((nz, 2, TOK, CH), BF16),
            v((nz, 2, CH, TOK), BF16),
            v((2 * nk, 2, nz, rowt, TOK), BF16),
            v((2 * nk, rowt, TOK), BF16),
            v((TOK, CH), BF16),
            v((TOK, CH), BF16),
            v((TOK, CH), BF16),
            v((TOK, STATE), BF16),
            v((TOK, STATE), BF16),
            v((2 * HALF, TOK), F32),
            v((2, TOK, CH), BF16),
            v((2, TOK, STATE), BF16),
            v((2, TOK, STATE), BF16),
            v((2, 2 * HALF, TOK), F32),
            v((1, TOK), F32),
            v((nz, 1, TOK), F32),
            v((2, nz, piece, STATE), BF16),
            v((2, nz, piece, STATE), BF16),
            v((2, nz, piece, STATE), BF16),
            v((2, nz, piece, STATE), BF16),
            v((2, CH, TOK), F32),
            v((2, CH, TOK), BF16),
            v((2, TOK, CH), BF16),
            v((2, TOK, CH), BF16),
            v((2, CH, TOK), BF16),
            v((2 * HALF, TOK, TOK), F32),
            v((2, TOK, TOK), F32),
            v((2, CH, TOK), F32),
            v((2, CH, TOK), F32),
            v((CH, STATE), F32),
            v((CH, STATE), F32),
            v((6, 2 * HALF, TOK), F32),
            v((2 * TOK, CH), BF16),
            v((2 * TOK, CH), F32),
            v((CH, 2 * TOK), F32),
            v((2, nk, 2, TOK, CH), BF16),
            v((nk, 2, TOK, CH), BF16),
            v((nk, 2, TOK, CH), BF16),
            v((chips, TOK, CH), BF16),
            v((2, 2, TOK // 2, STATE), F32),
            v((4, TOK // 2, STATE), F32),
            v((2 * nk, TOK // 2, STATE), BF16),
            v((2, 2 * HALF, TOK), F32),
            v((2 * HALF, TOK), F32),
            v((2, TOK, CH), BF16),
            pltpu.SemaphoreType.DMA((11,)),
            pltpu.SemaphoreType.DMA((25,)),
            pltpu.SemaphoreType.DMA((23 + 16 * (nz // 2 + 1),)),
        ],
        compiler_params=pltpu.CompilerParams(
            collective_id=0, has_side_effects=True, vmem_limit_bytes=60 * 1024 * 1024
        ),
        name="mixer_backward",
    )(tokens, w, cot, b, c, raw, rate_log.reshape(1, 2 * HALF), skip.reshape(1, 2 * HALF))

    def hand_over(*refs):
        for first in (0, 8):
            copies = [
                pltpu.make_async_copy(refs[(first + n) % 12], refs[8 - first // 2 + n], refs[12].at[n])
                for n in range(4)
            ]
            for copy in copies:
                copy.start()
            for copy in copies:
                copy.wait()

    return pl.pallas_call(
        hand_over,
        out_shape=tuple(jax.ShapeDtypeStruct(a.shape, a.dtype) for a in results),
        in_specs=[hbm] * 4,
        out_specs=(hbm,) * 4,
        scratch_shapes=[v(a.shape, a.dtype) for a in results] + [pltpu.SemaphoreType.DMA((4,))],
        compiler_params=pltpu.CompilerParams(vmem_limit_bytes=60 * 1024 * 1024),
        name="outputs",
    )(*results)


def solution(mesh):
    return jax.shard_map(
        local,
        mesh=mesh,
        in_specs=(
            P("tok", "ch"),
            P("tok", "ch"),
            P("tok", "ch"),
            P(None, "tok", None),
            P(None, "tok", None),
            P("ch", "tok"),
            P("ch"),
            P("ch"),
        ),
        out_specs=(P("tok", "ch"), P("tok", "ch"), P("ch", "tok"), P(None, "tok", None)),
        check_vma=False,
    )
```
